32 devices in a mesh: seq: 8 (over z, x), head: 4 (over y, core).
Axes of the slice: x: 2, y: 2, z: 4, core: 2. Of those that a mesh axis runs over, the one named last changes fastest.
Arguments:
- hidden: bfloat16 [4096, 2048], P(('seq', 'head')), may hold values from -6 to 6
- norm_gain: float32 [2048], replicated, may hold values from 0.5 to 1.5
- expert_choice: int32 [4096, 8], P(('seq', 'head')), may hold values from 0 to 15, all different within a row; in each aligned block of 128 rows (0 to 127, 128 to 255, ...) at most 72 rows name the same one
- route_weight: bfloat16 [4096, 8], P(('seq', 'head')), may hold values from 0.049804688 to 0.3984375
- gate_weight: bfloat16 [32, 2048, 384], P(('seq', 'head')), may hold values from -0.125 to 0.125
- up_weight: bfloat16 [32, 2048, 384], P(('seq', 'head')), may hold values from -0.125 to 0.125
- down_weight: bfloat16 [32, 384, 2048], P(('seq', 'head')), may hold values from -0.21875 to 0.21875
- layer_grad: bfloat16 [4096, 2048], P(('seq', 'head')), may hold values from -6 to 6
- scan_input: bfloat16 [4096, 2048], P('seq', 'head'), may hold values from -6 to 6
- state_input: bfloat16 [4096, 128], P('seq'), may hold values from -0.5 to 0.5
- state_output: bfloat16 [4096, 128], P('seq'), may hold values from -0.5 to 0.5
- log_decay: float32 [4096, 32], P('seq', 'head'), may hold values from -1.5 to 0
- skip_gain: float32 [32], P('head'), may hold values from 0.5 to 2
- out_weight: bfloat16 [2048, 2048], P(None, 'head'), may hold values from -0.125 to 0.125
Outputs:
- d_hidden: bfloat16 [4096, 2048], P(('seq', 'head'))
- d_norm_gain: float32 [2048], replicated
- d_route_weight: bfloat16 [4096, 8], P(('seq', 'head'))
- d_gate_weight: bfloat16 [32, 2048, 384], P(('seq', 'head'))
- d_up_weight: bfloat16 [32, 2048, 384], P(('seq', 'head'))
- d_down_weight: bfloat16 [32, 384, 2048], P(('seq', 'head'))
- d_out_weight: bfloat16 [2048, 2048], P('seq', 'head')
- d_scan_input: bfloat16 [4096, 2048], P('seq', 'head')
- d_state_input: float32 [4096, 128], P('seq')
- d_state_output: float32 [4096, 128], P('seq')
- d_log_decay: float32 [4096, 32], P('seq', 'head')
- d_skip_gain: float32 [32], P('head')
The draws below stay inside these ranges and needn't reach their ends.
Inputs may be any that keep to these rules, and one draw needn't show every extreme that they name: `expert_choice`: each row names 8 different experts. In each aligned block of 128 rows (the rows of one device) no expert is named by more than 72 rows, and in some block some expert is named by exactly 72 rows.
All inputs are finite; a program needn't handle non-finite values.
Results may differ from the reference program's by a relative error of at most 0.015.
Values may be sent and summed in bfloat16 or wider, within the bound.
No kernel may reach another device: no remote copies, remote signals or barrier semaphores. Data moves between devices by JAX's collectives and lax.ppermute only.
A program may use at most 256 MiB of HBM per device.

```python
import math
import jax
import jax.numpy as jnp
import numpy as np
from jax import lax

D = 2048
FF = 768
TOPK = 8
HEADS = 32
HEAD_DIM = 64
STATE = 128
SEQ_DEV = 512
SEQUENCE_LENGTH = 4096
TOK_DEV = 128
EXPERTS = 16
CAP = 72
N_SEQ = 8
N_HEAD = 4


def draw_log_decay(key, part):
    random_child_keys = jax.random.split(key, 7)
    blocks = SEQUENCE_LENGTH // SEQ_DEV
    fast_share = 0.5
    jitter_low = 0.5
    jitter_high = 1.5
    fast_heads = jax.random.uniform(random_child_keys[0], (HEADS,), jnp.float32) < fast_share
    fast_rate = jnp.exp(jax.random.uniform(random_child_keys[1], (HEADS,), jnp.float32, math.log(1.0 / 50.0), math.log(1.0 / 30.0)))
    slow_rate = jnp.exp(jax.random.uniform(random_child_keys[2], (HEADS,), jnp.float32, math.log(0.1), math.log(0.4))) / SEQUENCE_LENGTH
    head_decay_rate = jnp.where(fast_heads, fast_rate, slow_rate)
    multiplier = jnp.exp(jax.random.uniform(random_child_keys[3], (blocks, 1, HEADS), jnp.float32, math.log(0.6), math.log(1.5)))
    multiplier = jnp.broadcast_to(multiplier, (blocks, SEQ_DEV, HEADS)).reshape(SEQUENCE_LENGTH, HEADS)
    random_wobble = jax.random.uniform(random_child_keys[4], (SEQUENCE_LENGTH, HEADS), jnp.float32, jitter_low, jitter_high)
    spike_positions = jax.random.randint(random_child_keys[5], (2,), 0, SEQUENCE_LENGTH)
    loss_values = jax.random.uniform(random_child_keys[6], (2, HEADS), jnp.float32, 0.2, 0.5)
    spike_values = (jnp.arange(SEQUENCE_LENGTH)[:, None] == spike_positions[None, :]).astype(jnp.float32)
    return -head_decay_rate[None, :] * multiplier * random_wobble + jnp.dot(spike_values, jnp.log(1.0 - loss_values))


def strengthened(values, stream_key, source, target, parts, factor):
    owner, partner = [(jnp.arange(values.shape[dim]) // (values.shape[dim] // parts)).reshape([-1 if axis == dim else 1 for axis in range(values.ndim)]) for dim in (source, target)]
    chosen = jax.random.permutation(stream_key, parts)[partner]
    strong = (owner == chosen) | (owner == (partner + parts // 2) % parts)
    return jnp.where(strong, factor * values, values)


def shard_levels(stream_key, dims, cuts, low, high):
    level, own = 1.0, jax.random.fold_in(stream_key, 6)
    for dim, shards_of in cuts:
        draws = jnp.exp(jax.random.uniform(jax.random.fold_in(own, dim), (shards_of,), jnp.float32, low / len(cuts), high / len(cuts)))
        level = level * jnp.repeat(draws, dims[dim] // shards_of).reshape([-1 if axis == dim else 1 for axis in range(len(dims))])
    return level


def shared_out(own_key, own, number, rows, number_of, top, limit, slope):
    sequence = jax.random.permutation(own_key, number_of)
    packed, usual = load_shares(number_of, rows * top, limit, slope, True), load_shares(number_of, rows * top, limit, slope, False)
    places = jnp.arange(number_of)

    def named(tallies, rotation):
        used = int((tallies > 0).sum())
        fixed = max(1, used // 4)
        shifted = fixed + (places - fixed + rotation * (used - fixed)) % max(1, number_of - fixed)
        return jnp.zeros((number_of,), jnp.int32).at[sequence[jnp.where(places < fixed, places, shifted)]].set(jnp.asarray(tallies, jnp.int32))

    tallies = jnp.where(number % 4 == 0, named(packed, number // 4), named(usual, number - number // 4 - 1))
    mixed = jax.random.permutation(jax.random.fold_in(own, 3), number_of)
    source_of, sink = mixed[0:number_of // 2 * 2:2], mixed[1:number_of // 2 * 2:2]
    slack = jnp.minimum(tallies[source_of] - 1, limit - tallies[sink]) // 2
    slack = jnp.where((source_of == sequence[0]) | (sink == sequence[0]) | (tallies[sink] == 0), 0, jnp.maximum(slack, 0))
    shifted = jax.random.randint(jax.random.fold_in(own, 4), (number_of // 2,), 0, 1 << 20) % (slack + 1)
    tallies = tallies.at[source_of].add(-shifted).at[sink].add(shifted)
    labels = jnp.searchsorted(jnp.cumsum(tallies), jnp.arange(rows * top), side="right").astype(jnp.int32)
    table = labels.reshape(top, rows).T
    table = table[jax.random.permutation(jax.random.fold_in(own, 1), rows)]
    rotation = jax.random.randint(jax.random.fold_in(own, 2), (rows, 1), 0, top)
    return jnp.take_along_axis(table, (jnp.arange(top)[None, :] + rotation) % top, axis=1)


def load_shares(number_of, total, bound, skew, full):
    loads = [(1 << 20) // math.isqrt(grade ** skew) + 1 for grade in range(1, number_of + 1)]
    largest = bound if full else min(bound, max(-(-total // number_of), total * loads[0] // sum(loads)))
    least = 1 if total - largest >= number_of - 1 else 0
    holding, rest = [largest] + [least] * (number_of - 1), total - largest - least * (number_of - 1)
    while rest > 0:
        movable = [i for i in range(1, number_of) if holding[i] < largest] or [i for i in range(1, number_of) if holding[i] < bound]
        pool, budget = sum([loads[i] for i in movable]), rest
        for i in movable:
            extra = min(bound - holding[i], max(1, budget * loads[i] // pool), rest)
            holding[i] = holding[i] + extra
            rest = rest - extra
    return np.array(holding)


def gaussian(own_key, dims, scale, bound, cuts=(), held_as=jnp.bfloat16):
    array = scale * jax.random.normal(own_key, dims, jnp.float32)
    if cuts:
        array = array * shard_levels(own_key, dims, cuts, -0.22, 0.18)
    return jnp.clip(array, -bound, bound).astype(held_as)


def gaussian_with(rng, extent, width, most, shards, heavy, kind=jnp.bfloat16):
    values = width * jax.random.normal(rng, extent, jnp.float32)
    if shards:
        values = values * shard_levels(rng, extent, shards, -0.22, 0.18)
    return jnp.clip(strengthened(values, jax.random.fold_in(rng, 3), *heavy), -most, most).astype(kind)


def setup_inputs(seed: int = 0) -> dict:
    streams_of = jax.random.split(jax.random.key(seed), 15)
    hidden = gaussian(streams_of[0], (SEQUENCE_LENGTH, D), 1.0, 6.0, ((0, 32),))
    norm_gain = jnp.clip(1.0 + 0.1 * jax.random.normal(streams_of[1], (D,), jnp.float32), 0.5, 1.5)
    expert_choice_keys = jax.random.split(jax.random.fold_in(streams_of[2], 1), SEQUENCE_LENGTH // TOK_DEV)
    expert_choice_turns = jax.random.permutation(jax.random.fold_in(streams_of[2], 3), SEQUENCE_LENGTH // TOK_DEV)
    expert_choice = jax.vmap(lambda own, number: shared_out(jax.random.fold_in(streams_of[2], 2), own, number, TOK_DEV, EXPERTS, TOPK, CAP, 2))(expert_choice_keys, expert_choice_turns).reshape((SEQUENCE_LENGTH, TOPK))
    route_weight = jnp.clip(0.049804688 + 0.3486328 * jax.random.uniform(streams_of[3], (SEQUENCE_LENGTH, TOPK), jnp.float32) ** shard_levels(streams_of[3], (SEQUENCE_LENGTH, TOPK), ((0, 32),), -0.2, 0.2), 0.049804688, 0.3984375).astype(jnp.bfloat16)
    gate_weight = gaussian(streams_of[4], (2 * EXPERTS, D, FF // 2), D ** -0.5, 0.125, ((0, 32),))
    up_weight = gaussian(streams_of[5], (2 * EXPERTS, D, FF // 2), D ** -0.5, 0.125, ((0, 32),))
    down_weight = gaussian(streams_of[6], (2 * EXPERTS, FF // 2, D), FF ** -0.5, 0.21875, ((0, 32),))
    layer_grad = gaussian_with(streams_of[7], (SEQUENCE_LENGTH, D), 0.5, 6.0, ((0, 32),), (0, 1, 32, 2.75))
    scan_input = gaussian(streams_of[8], (SEQUENCE_LENGTH, HEADS * HEAD_DIM), 1.0, 6.0, ((0, 8), (1, 4)))
    state_input = gaussian(streams_of[9], (SEQUENCE_LENGTH, STATE), STATE ** -0.5, 0.5, ((0, 8),))
    state_output = gaussian(streams_of[10], (SEQUENCE_LENGTH, STATE), STATE ** -0.5, 0.5, ((0, 8),))
    log_decay = draw_log_decay(jax.random.fold_in(streams_of[14], 71), 0)
    skip_gain = jnp.clip(jnp.exp(math.log(2.0) - 1.3862944 * jax.random.uniform(streams_of[12], (HEADS,), jnp.float32) ** shard_levels(streams_of[12], (HEADS,), ((0, 4),), -0.2, 0.2)), 0.5, 2.0)
    out_weight = gaussian(streams_of[13], (D, HEADS * HEAD_DIM), (HEADS * HEAD_DIM) ** -0.5, 0.125, ((1, 4),))
    return dict(hidden=hidden, norm_gain=norm_gain, expert_choice=expert_choice, route_weight=route_weight, gate_weight=gate_weight, up_weight=up_weight, down_weight=down_weight, layer_grad=layer_grad, scan_input=scan_input, state_input=state_input, state_output=state_output, log_decay=log_decay, skip_gain=skip_gain, out_weight=out_weight)


highest = lax.Precision.HIGHEST
epsilon = 1e-06

def expert_rows(normed_rows, grad_rows, prob_rows, gate_full, up_full, down_full):
    normed_wide = normed_rows.astype(jnp.float32)
    grad_wide = grad_rows.astype(jnp.float32)
    gate_wide = gate_full.astype(jnp.float32)
    up_wide = up_full.astype(jnp.float32)
    down_wide = down_full.astype(jnp.float32)
    gate_pre = jnp.dot(normed_wide, gate_wide)
    up_pre = jnp.dot(normed_wide, up_wide)
    gate_sig = jax.nn.sigmoid(gate_pre)
    active = lax.optimization_barrier((gate_pre * gate_sig * up_pre).astype(jnp.bfloat16)).astype(jnp.float32)
    back_grad = jnp.dot(grad_wide, down_wide.T)
    weight_column = prob_rows.astype(jnp.float32)[:, None]
    prob_part = lax.optimization_barrier(jnp.sum(active * back_grad, axis=1))
    d_active = weight_column * back_grad
    scaled = lax.optimization_barrier((weight_column * grad_wide).astype(jnp.bfloat16)).astype(jnp.float32)
    d_gate = lax.optimization_barrier((d_active * up_pre * gate_sig * (1.0 + gate_pre * (1.0 - gate_sig))).astype(jnp.bfloat16)).astype(jnp.float32)
    d_up = lax.optimization_barrier((d_active * gate_pre * gate_sig).astype(jnp.bfloat16)).astype(jnp.float32)
    gate_term = jnp.dot(normed_wide.T, d_gate)
    up_term = jnp.dot(normed_wide.T, d_up)
    down_term = jnp.dot(active.T, scaled)
    row_part = jnp.dot(d_gate, gate_wide.T) + jnp.dot(d_up, up_wide.T)
    return (gate_term, up_term, down_term, row_part, prob_part)

def ssd_forward(scan_values, input_rows, output_rows, decay_rows, skip_rows):
    blocks = SEQUENCE_LENGTH // SEQ_DEV
    lower_mask = jnp.arange(SEQ_DEV)[:, None] >= jnp.arange(SEQ_DEV)[None, :]

    def block_step(carried_state, block_data):
        block_values, block_inputs, block_outputs, block_decay = block_data
        cumulative = jnp.cumsum(block_decay, axis=0)
        spread = cumulative.T[:, :, None] - cumulative.T[:, None, :]
        decay_mask = jnp.where(lower_mask[None], jnp.exp(jnp.where(lower_mask[None], spread, 0.0)), 0.0)
        scores = jnp.dot(block_outputs, block_inputs.T, precision=highest)
        kernel = decay_mask * scores[None]
        read_state = jnp.einsum('tn,hnp->thp', block_outputs, carried_state, precision=highest)
        result = jnp.einsum('hts,shp->thp', kernel, block_values, precision=highest) + jnp.exp(cumulative)[:, :, None] * read_state
        to_end = jnp.exp(cumulative[-1][None, :] - cumulative)
        new_state = jnp.exp(cumulative[-1])[:, None, None] * carried_state + jnp.einsum('sn,shp->hnp', block_inputs, block_values * to_end[:, :, None], precision=highest)
        return (new_state, result)
    shaped = (scan_values.reshape(blocks, SEQ_DEV, HEADS, HEAD_DIM), input_rows.reshape(blocks, SEQ_DEV, STATE), output_rows.reshape(blocks, SEQ_DEV, STATE), decay_rows.reshape(blocks, SEQ_DEV, HEADS))
    last_state, results = lax.scan(jax.checkpoint(block_step), jnp.zeros((HEADS, STATE, HEAD_DIM), jnp.float32), shaped)
    return results.reshape(SEQUENCE_LENGTH, HEADS, HEAD_DIM) + skip_rows[None, :, None] * scan_values

def reference(hidden, norm_gain, expert_choice, route_weight, gate_weight, up_weight, down_weight, layer_grad, scan_input, state_input, state_output, log_decay, skip_gain, out_weight):
    hidden_wide = hidden.astype(jnp.float32)
    inverse = lax.rsqrt(lax.optimization_barrier(jnp.mean(hidden_wide * hidden_wide, axis=1, keepdims=True)) + epsilon)
    normalized = hidden_wide * inverse
    normed = (normalized * norm_gain[None, :]).astype(jnp.bfloat16)
    devices = N_SEQ * N_HEAD
    slot_count = TOK_DEV * TOPK
    blocks = expert_choice.reshape(devices, slot_count)
    chosen = (blocks[:, :, None] == jnp.arange(EXPERTS, dtype=jnp.int32)[None, None, :]).astype(jnp.int32)
    position = lax.optimization_barrier(jnp.sum((jnp.cumsum(chosen, axis=1) - chosen) * chosen, axis=2)).astype(jnp.int32)
    column = jnp.arange(devices, dtype=jnp.int32)[:, None] * CAP + position
    slot_index = jnp.arange(devices * slot_count, dtype=jnp.int32).reshape(devices, slot_count)
    slot_table = jnp.full((EXPERTS, devices * CAP), SEQUENCE_LENGTH * TOPK, jnp.int32).at[blocks, column].set(slot_index)
    token_table = (slot_table // TOPK).astype(jnp.int32)
    normed_pad = jnp.concatenate([normed, jnp.zeros((1, D), jnp.bfloat16)], axis=0)
    grad_pad = jnp.concatenate([layer_grad, jnp.zeros((1, D), jnp.bfloat16)], axis=0)
    prob_pad = jnp.concatenate([route_weight.reshape(-1), jnp.zeros((1,), jnp.bfloat16)], axis=0)
    gate_split = gate_weight.reshape(EXPERTS, 2, D, FF // 2)
    up_split = up_weight.reshape(EXPERTS, 2, D, FF // 2)
    down_split = down_weight.reshape(EXPERTS, FF, D)

    def per_expert(totals, inputs):
        row_total, prob_total = totals
        tokens, slots, gate_pair, up_pair, down_full = inputs
        gate_full = jnp.concatenate([gate_pair[0], gate_pair[1]], axis=1)
        up_full = jnp.concatenate([up_pair[0], up_pair[1]], axis=1)
        expert_terms = expert_rows(normed_pad[tokens], grad_pad[tokens], prob_pad[slots], gate_full, up_full, down_full)
        rounded_rows = lax.optimization_barrier(expert_terms[3].astype(jnp.bfloat16)).astype(jnp.float32)
        row_total = row_total.at[tokens].add(rounded_rows)
        prob_total = prob_total.at[slots].add(expert_terms[4])
        return ((row_total, prob_total), (expert_terms[0].astype(jnp.bfloat16), expert_terms[1].astype(jnp.bfloat16), expert_terms[2].astype(jnp.bfloat16)))
    start_totals = (jnp.zeros((SEQUENCE_LENGTH + 1, D), jnp.float32), jnp.zeros((SEQUENCE_LENGTH * TOPK + 1,), jnp.float32))
    (row_total, prob_total), weights = lax.scan(per_expert, start_totals, (token_table, slot_table, gate_split, up_split, down_split))
    d_gate_weight = weights[0].reshape(EXPERTS, D, 2, FF // 2).transpose(0, 2, 1, 3).reshape(2 * EXPERTS, D, FF // 2)
    d_up_weight = weights[1].reshape(EXPERTS, D, 2, FF // 2).transpose(0, 2, 1, 3).reshape(2 * EXPERTS, D, FF // 2)
    d_down_weight = weights[2].reshape(2 * EXPERTS, FF // 2, D)
    d_normed = row_total[:SEQUENCE_LENGTH]
    d_route_weight = prob_total[:SEQUENCE_LENGTH * TOPK].reshape(SEQUENCE_LENGTH, TOPK).astype(jnp.bfloat16)
    gain_scaled = norm_gain[None, :] * d_normed
    centered = lax.optimization_barrier(jnp.mean(gain_scaled * normalized, axis=1, keepdims=True))
    d_hidden = (layer_grad.astype(jnp.float32) + inverse * (gain_scaled - normalized * centered)).astype(jnp.bfloat16)
    d_norm_gain = lax.optimization_barrier(jnp.sum(d_normed * normalized, axis=0))
    grad_rounded = jnp.dot(d_hidden, out_weight, preferred_element_type=jnp.float32).astype(jnp.bfloat16)
    scan_values = scan_input.astype(jnp.float32).reshape(SEQUENCE_LENGTH, HEADS, HEAD_DIM)
    y_values, pullback = jax.vjp(ssd_forward, scan_values, state_input.astype(jnp.float32), state_output.astype(jnp.float32), log_decay, skip_gain)
    y_rounded = y_values.reshape(SEQUENCE_LENGTH, HEADS * HEAD_DIM).astype(jnp.bfloat16)
    d_out_weight = jnp.dot(d_hidden.T, y_rounded, preferred_element_type=jnp.float32).astype(jnp.bfloat16)
    gradients = pullback(grad_rounded.astype(jnp.float32).reshape(SEQUENCE_LENGTH, HEADS, HEAD_DIM))
    d_scan_input = gradients[0].reshape(SEQUENCE_LENGTH, HEADS * HEAD_DIM).astype(jnp.bfloat16)
    return (d_hidden, d_norm_gain, d_route_weight, d_gate_weight, d_up_weight, d_down_weight, d_out_weight, d_scan_input, gradients[1], gradients[2], gradients[3], gradients[4])
```

```python
import functools

import jax
import jax.numpy as jnp
from jax import lax
from jax.experimental import pallas as pl
from jax.experimental.pallas import tpu as pltpu
from jax.sharding import PartitionSpec as P

highest = lax.Precision.HIGHEST
epsilon = 1e-06
wide = jnp.float32
short = jnp.bfloat16
both = ("seq", "head")
parts_count = 2


def log2(number):
    return number.bit_length() - 1


def flipped(value, axis, mask):
    names = axis if isinstance(axis, tuple) else (axis,)
    size = 1
    for name in names:
        size = size * lax.axis_size(name)
    return lax.ppermute(value, axis, [(i, i ^ mask) for i in range(size)])


def shifted(value, axis, distance):
    size = lax.axis_size(axis)
    pairs = [(i, i + distance) for i in range(size) if 0 <= i + distance < size]
    return lax.ppermute(value, axis, pairs)


def summed(value, axis):
    size = lax.axis_size(axis)
    for bit in range(log2(size)):
        value = value + flipped(value, axis, 1 << bit)
    return value


def dot_nn(a, b, out=wide):
    return lax.dot_general(a, b, (((1,), (0,)), ((), ())), preferred_element_type=out)


def dot_nt(a, b, out=wide):
    return lax.dot_general(a, b, (((1,), (1,)), ((), ())), preferred_element_type=out)


def dot_tn(a, b, out=wide):
    return lax.dot_general(a, b, (((0,), (0,)), ((), ())), preferred_element_type=out)


def forward_kernel(heads, b_ref, c_ref, x_ref, row_ref, col_ref, y_ref, score_ref):
    step = pl.program_id(0)
    rows = b_ref.shape[0]

    @pl.when(step == 0)
    def _():
        score_ref[...] = dot_nt(c_ref[...], b_ref[...])

    scores = score_ref[...]
    keep = lax.broadcasted_iota(jnp.int32, (rows, rows), 0) >= lax.broadcasted_iota(
        jnp.int32, (rows, rows), 1
    )
    block = x_ref[...]
    width = block.shape[1]
    lane = lax.broadcasted_iota(jnp.int32, (rows, width), 1)
    head_lane = lax.broadcasted_iota(jnp.int32, col_ref.shape, 1)
    total = jnp.zeros((rows, width), wide)
    for k in range(heads):
        head = step * heads + k
        column = jnp.sum(jnp.where(head_lane == head, col_ref[...], 0.0), axis=1, keepdims=True)
        line = row_ref[pl.ds(head, 1), :]
        decay = jnp.where(keep, jnp.exp(jnp.minimum(column - line, 0.0)), 0.0)
        mine = (lane // (width // heads)) == k
        total = total + dot_nn(
            (decay * scores).astype(short), jnp.where(mine, block, jnp.zeros_like(block))
        )
    y_ref[...] = total


def backward_kernel(
    heads, b_ref, c_ref, x_ref, g_ref, row_ref, col_ref,
    dx_ref, tsum_ref, ssum_ref, db_ref, dc_ref, score_ref, mask_ref,
):
    step = pl.program_id(0)
    rows = b_ref.shape[0]

    @pl.when(step == 0)
    def _():
        score_ref[...] = dot_nt(b_ref[...], c_ref[...])
        mask_ref[...] = jnp.zeros_like(mask_ref)
        ssum_ref[...] = jnp.zeros_like(ssum_ref)

    scores = score_ref[...]
    keep = lax.broadcasted_iota(jnp.int32, (rows, rows), 0) <= lax.broadcasted_iota(
        jnp.int32, (rows, rows), 1
    )
    values = x_ref[...]
    grads = g_ref[...]
    width = values.shape[1]
    lane = lax.broadcasted_iota(jnp.int32, (rows, width), 1)
    head_lane = lax.broadcasted_iota(jnp.int32, col_ref.shape, 1)
    total = jnp.zeros((rows, width), wide)
    for k in range(heads):
        head = step * heads + k
        column = jnp.sum(jnp.where(head_lane == head, col_ref[...], 0.0), axis=1, keepdims=True)
        line = row_ref[pl.ds(head, 1), :]
        decay = jnp.where(keep, jnp.exp(jnp.minimum(line - column, 0.0)), 0.0)
        mine = (lane // (width // heads)) == k
        head_grads = jnp.where(mine, grads, jnp.zeros_like(grads))
        pair = decay * dot_nt(values, head_grads)
        mask_ref[...] += pair
        full = pair * scores
        tsum_ref[pl.ds(head, 1), :] = jnp.sum(full, axis=0, keepdims=True)
        ssum_ref[...] += jnp.where(head_lane == head, jnp.sum(full, axis=1, keepdims=True), 0.0)
        total = total + dot_nn((decay * scores).astype(short), head_grads)
    dx_ref[...] = total

    @pl.when(step == pl.num_programs(0) - 1)
    def _():
        mask = mask_ref[...].astype(short)
        db_ref[...] = dot_nn(mask, c_ref[...])
        dc_ref[...] = dot_tn(mask, b_ref[...])


def scan_blocks(rows, state, width, heads_local):
    whole = pl.BlockSpec((rows, state), lambda i: (0, 0))
    column = pl.BlockSpec((rows, width), lambda i: (0, i))
    lines = pl.BlockSpec((heads_local, rows), lambda i: (0, 0))
    columns = pl.BlockSpec((rows, heads_local), lambda i: (0, 0))
    return whole, column, lines, columns


def scan_forward(b, c, x, lines, columns):
    rows, state = b.shape
    inner = x.shape[1]
    heads_local = columns.shape[1]
    width = 2 * (inner // heads_local)
    whole, column, line_spec, column_spec = scan_blocks(rows, state, width, heads_local)
    return pl.pallas_call(
        functools.partial(forward_kernel, 2),
        grid=(heads_local // 2,),
        in_specs=[whole, whole, column, line_spec, column_spec],
        out_specs=column,
        out_shape=jax.ShapeDtypeStruct((rows, inner), wide),
        scratch_shapes=[pltpu.VMEM((rows, rows), wide)],
        compiler_params=pltpu.CompilerParams(vmem_limit_bytes=24 * 1024 * 1024),
        cost_estimate=pl.CostEstimate(
            flops=4 * rows * rows * 128 * heads_local,
            bytes_accessed=rows * inner * 6 + rows * state * 4,
            transcendentals=rows * rows * heads_local,
        ),
    )(b, c, x, lines, columns)


def scan_backward(b, c, x, g, lines, columns):
    rows, state = b.shape
    inner = x.shape[1]
    heads_local = columns.shape[1]
    width = 2 * (inner // heads_local)
    whole, column, line_spec, column_spec = scan_blocks(rows, state, width, heads_local)
    return pl.pallas_call(
        functools.partial(backward_kernel, 2),
        grid=(heads_local // 2,),
        in_specs=[whole, whole, column, column, line_spec, column_spec],
        out_specs=[column, line_spec, column_spec, whole, whole],
        out_shape=[
            jax.ShapeDtypeStruct((rows, inner), wide),
            jax.ShapeDtypeStruct((heads_local, rows), wide),
            jax.ShapeDtypeStruct((rows, heads_local), wide),
            jax.ShapeDtypeStruct((rows, state), wide),
            jax.ShapeDtypeStruct((rows, state), wide),
        ],
        scratch_shapes=[pltpu.VMEM((rows, rows), wide), pltpu.VMEM((rows, rows), wide)],
        compiler_params=pltpu.CompilerParams(vmem_limit_bytes=32 * 1024 * 1024),
        cost_estimate=pl.CostEstimate(
            flops=8 * rows * rows * 128 * heads_local,
            bytes_accessed=rows * inner * 8 + rows * state * 12,
            transcendentals=rows * rows * heads_local,
        ),
    )(b, c, x, g, lines, columns)


def shards(
    hidden,
    norm_gain,
    expert_choice,
    route_weight,
    gate_weight,
    up_weight,
    down_weight,
    layer_grad,
    scan_input,
    state_input,
    state_output,
    log_decay,
    skip_gain,
    out_weight,
):
    seq_size, head_size = lax.axis_size("seq"), lax.axis_size("head")
    devices = seq_size * head_size
    experts = devices // 2
    tok, model_width = hidden.shape
    top_count = expert_choice.shape[1]
    half = 9 * tok * top_count // (16 * experts)
    groups = 1 << ((log2(devices)) // 2)
    plane = devices // groups
    plane_experts = plane // 2
    seq_place, head_place = lax.axis_index("seq"), lax.axis_index("head")
    place = seq_place * head_size + head_place
    group = place // plane
    plane_lists = [[z * plane + j for j in range(plane)] for z in range(groups)]

    def across(value, mask):
        return flipped(value, both, mask * plane)

    def spread(first):
        rows = [first]
        for m in range(1, groups):
            low = m & -m
            rows.append(across(rows[m ^ low], low))
        return rows

    def exchanged(value):
        return lax.all_to_all(
            value, both, split_axis=0, concat_axis=0, tiled=True, axis_index_groups=plane_lists
        )

    choice_t = expert_choice.T
    named = choice_t[None, :, :] == jnp.arange(experts, dtype=jnp.int32)[:, None, None]
    chosen = jnp.any(named, axis=1)
    before = jnp.arange(tok)[:, None] < jnp.arange(tok)[None, :]
    rank = dot_nn(chosen.astype(short), before.astype(short))
    rank = jnp.where(chosen, rank, -1.0)
    prob = jnp.sum(jnp.where(named, route_weight.T.astype(wide)[None], 0.0), axis=1)
    tables = spread(jnp.concatenate([rank, prob], axis=0))

    hidden_wide = hidden.astype(wide)
    inverse = lax.rsqrt(jnp.mean(hidden_wide * hidden_wide, axis=1, keepdims=True) + epsilon)
    normalized = hidden_wide * inverse
    normed = (normalized * norm_gain[None, :]).astype(short)
    normed_rows = spread(normed)
    grad_rows = spread(layer_grad)

    gate_up = jnp.concatenate([gate_weight[0], up_weight[0]], axis=1)
    weights = [(gate_up, down_weight[0])]
    weights.append((flipped(gate_up, "head", 1), flipped(down_weight[0], "head", 1)))
    hidden_half = down_weight.shape[1]

    per_part = groups // parts_count
    slot_rows = per_part * half
    onehots, probs, sent_normed, sent_grad = [], [], [], []
    for part in range(parts_count):
        members = range(part * per_part, (part + 1) * per_part)
        ranks, part_probs = [], []
        for b, m in enumerate(members):
            first = group * plane_experts
            mine = lax.dynamic_slice_in_dim(tables[m], first, plane_experts, 0)
            weight = lax.dynamic_slice_in_dim(tables[m], experts + first, plane_experts, 0)
            mine = jnp.stack([mine, mine - half], axis=1).reshape(plane, tok)
            ranks.append(jnp.where((mine >= 0) & (mine < half), mine + b * half, -1.0))
            part_probs.append(jnp.stack([weight, weight], axis=1).reshape(plane, tok))
        target = jnp.concatenate(ranks, axis=1).astype(jnp.int32)
        weight = jnp.concatenate(part_probs, axis=1)
        table = target[:, None, :] == jnp.arange(slot_rows, dtype=jnp.int32)[None, :, None]
        probs.append(jnp.sum(jnp.where(table, weight[:, None, :], 0.0), axis=2))
        onehot = table.astype(short).reshape(plane * slot_rows, per_part * tok)
        onehots.append(onehot)
        part_normed = jnp.concatenate([normed_rows[m] for m in members], axis=0)
        part_grad = jnp.concatenate([grad_rows[m] for m in members], axis=0)
        sent_normed.append(dot_nn(onehot, part_normed, short).reshape(plane, slot_rows, model_width))
        sent_grad.append(dot_nn(onehot, part_grad, short).reshape(plane, slot_rows, model_width))
    received = []
    for part in range(parts_count):
        received.append([exchanged(sent_normed[part]), exchanged(sent_grad[part])])
    prob_slots = exchanged(jnp.concatenate(probs, axis=1)[:, None, :])
    prob_slots = prob_slots.reshape(plane, parts_count, slot_rows).transpose(1, 0, 2)

    seq_rows, inner_width = scan_input.shape
    heads_local = log_decay.shape[1]
    head_dim = inner_width // heads_local
    lower = jnp.arange(seq_rows)[:, None] >= jnp.arange(seq_rows)[None, :]
    lower_ones = lower.astype(wide)
    cumulative = jnp.dot(lower_ones, log_decay, precision=highest)
    cumulative_t = cumulative.T
    total_decay = cumulative[-1]
    head_of = (jnp.arange(inner_width) // head_dim)[None, :] == jnp.arange(heads_local)[:, None]
    expand = head_of.astype(wide)

    def expanded(value):
        return jnp.repeat(value, head_dim, axis=1)

    from_start = expanded(jnp.exp(cumulative))
    to_end = expanded(jnp.exp(total_decay[None, :] - cumulative))
    skip_row = jnp.repeat(skip_gain, head_dim)[None, :]
    values = scan_input.astype(wide)
    values_end = (values * to_end).astype(short)
    inner_seq = 1 << (log2(seq_size) // 2)
    outer_seq = seq_size // inner_seq
    inner_place, outer_place = seq_place % inner_seq, seq_place // inner_seq

    line = total_decay[None, :]
    pieces = jnp.concatenate([line] + [flipped(line, "seq", m) for m in range(1, inner_seq)], axis=0)
    pieces = jnp.take(pieces, jnp.arange(inner_seq) ^ inner_place, axis=0)
    pieces = jnp.stack(
        [pieces] + [flipped(pieces, "seq", m * inner_seq) for m in range(1, outer_seq)], axis=0
    )
    totals = jnp.take(pieces, jnp.arange(outer_seq) ^ outer_place, axis=0).reshape(seq_size, heads_local)
    reached = jnp.cumsum(totals, axis=0)
    ended = jnp.concatenate([jnp.zeros((1, heads_local), wide), reached], axis=0)

    def before_of(index):
        return lax.dynamic_index_in_dim(ended, jnp.clip(index, 0, seq_size), 0, False)

    def factor(log_value):
        return jnp.repeat(jnp.exp(jnp.minimum(log_value, 0.0)), head_dim)[:, None]

    def carried(local, reverse):
        start = outer_place * inner_seq
        pieces = [local] + [flipped(local, "seq", m) for m in range(1, inner_seq)]
        nearby = jnp.zeros(local.shape, wide)
        joined = jnp.zeros(local.shape, wide)
        for m in range(inner_seq):
            source = start + (inner_place ^ m)
            value = pieces[m].astype(wide)
            if reverse:
                near = before_of(source) - before_of(seq_place + 1)
                far = before_of(source) - before_of(start)
                ahead = source > seq_place
            else:
                near = before_of(seq_place) - before_of(source + 1)
                far = before_of(start + inner_seq) - before_of(source + 1)
                ahead = source < seq_place
            nearby = nearby + jnp.where(ahead, factor(near), 0.0) * value
            joined = joined + factor(far) * value
        joined = joined.astype(short)
        for k in range(1, outer_seq):
            if reverse:
                other = shifted(joined, "seq", -k * inner_seq)
                log_value = before_of(start + k * inner_seq) - before_of(seq_place + 1)
            else:
                other = shifted(joined, "seq", k * inner_seq)
                log_value = before_of(seq_place) - before_of(start - (k - 1) * inner_seq)
            nearby = nearby + factor(log_value) * other.astype(wide)
        return nearby

    local_state = dot_tn(values_end, state_input, short)
    state_in = carried(local_state, False)
    state_short = state_in.astype(short)
    read_state = dot_nt(state_output, state_short) * from_start
    y_inner = scan_forward(state_input, state_output, scan_input, cumulative_t, cumulative)
    y_rounded = (y_inner + read_state + skip_row * values).astype(short)

    def activated(part):
        rows = received[part][0].reshape(plane * slot_rows, model_width)
        grads = received[part][1].reshape(plane * slot_rows, model_width)
        weight_column = prob_slots[part].reshape(-1)[:, None]
        prob_total, row_total, halves = 0.0, 0.0, []
        for gate_up_half, down_half in weights:
            pre = dot_nn(rows, gate_up_half)
            gate_pre, up_pre = pre[:, :hidden_half], pre[:, hidden_half:]
            sig = jax.nn.sigmoid(gate_pre)
            active = (gate_pre * sig * up_pre).astype(short)
            back = dot_nt(grads, down_half)
            prob_total = prob_total + jnp.sum(active.astype(wide) * back, axis=1)
            d_active = weight_column * back
            d_gate = (d_active * up_pre * sig * (1.0 + gate_pre * (1.0 - sig))).astype(short)
            d_up = (d_active * gate_pre * sig).astype(short)
            d_pre = jnp.concatenate([d_gate, d_up], axis=1)
            row_total = row_total + dot_nt(d_pre, gate_up_half)
            halves.append((active, d_pre))
        scaled = (weight_column * grads.astype(wide)).astype(short)
        return row_total.astype(short), prob_total, halves, rows, scaled

    done = [activated(part) for part in range(parts_count)]
    partial = [None] * groups
    prob_partial = [None] * groups
    returned_prob = exchanged(
        jnp.stack([done[part][1].reshape(plane, slot_rows) for part in range(parts_count)], axis=1)
    )
    for part in reversed(range(parts_count)):
        back = exchanged(done[part][0].reshape(plane, slot_rows, model_width))
        back = back.reshape(plane * slot_rows, model_width)
        token_sum = dot_tn(onehots[part], back)
        table = onehots[part].reshape(plane, slot_rows, per_part * tok).astype(wide)
        prob_sum = jnp.sum(table * returned_prob[:, part, :, None], axis=1)
        prob_sum = prob_sum.reshape(plane_experts, 2, per_part * tok).sum(axis=1)
        for b in range(per_part):
            index = part * per_part + b
            partial[index] = token_sum[b * tok : (b + 1) * tok]
            prob_partial[index] = prob_sum[:, b * tok : (b + 1) * tok]

    bit = 1
    tree = {m: partial[m] for m in range(groups)}
    while bit < groups:
        moved = {m: across(tree[m].astype(short), bit) for m in tree if m & bit}
        tree = {m: tree[m] + moved[m ^ bit].astype(wide) for m in tree if not m & bit}
        bit = bit * 2
    d_normed = tree[0]
    prob_all = jnp.stack(
        [prob_partial[0]] + [across(prob_partial[m], m) for m in range(1, groups)], axis=0
    )
    prob_all = jnp.take(prob_all, jnp.arange(groups) ^ group, axis=0).reshape(experts, tok)
    d_route_weight = jnp.sum(jnp.where(named, prob_all[:, None, :], 0.0), axis=0).T.astype(short)

    gain_scaled = norm_gain[None, :] * d_normed
    centered = jnp.mean(gain_scaled * normalized, axis=1, keepdims=True)
    d_hidden = (
        layer_grad.astype(wide) + inverse * (gain_scaled - normalized * centered)
    ).astype(short)
    d_norm_gain = jnp.sum(d_normed * normalized, axis=0)
    for axis in ("head", "seq"):
        d_norm_gain = summed(d_norm_gain, axis)

    rows_all = jnp.concatenate([done[part][3] for part in range(parts_count)], axis=0)
    scaled_all = jnp.concatenate([done[part][4] for part in range(parts_count)], axis=0)
    terms = []
    for side in (1, 0):
        active_all = jnp.concatenate([done[part][2][side][0] for part in range(parts_count)], axis=0)
        pre_all = jnp.concatenate([done[part][2][side][1] for part in range(parts_count)], axis=0)
        terms.append((dot_tn(rows_all, pre_all), dot_tn(active_all, scaled_all)))
    other_gate_up = flipped(terms[0][0].astype(short), "head", 1).astype(wide)
    other_down = flipped(terms[0][1].astype(short), "head", 1).astype(wide)
    d_gate_up = (terms[1][0] + other_gate_up).astype(short)
    d_gate_weight = d_gate_up[:, :hidden_half][None]
    d_up_weight = d_gate_up[:, hidden_half:][None]
    d_down_weight = (terms[1][1] + other_down).astype(short)[None]

    gathered = [d_hidden]
    order = [0]
    for k in reversed(range(log2(head_size))):
        gathered = gathered + [flipped(value, "head", 1 << k) for value in gathered]
        order = order + [m ^ (1 << k) for m in order]
    sorted_blocks = [None] * head_size
    for value, m in zip(gathered, order):
        sorted_blocks[m] = value
    cotangent = jnp.concatenate(sorted_blocks, axis=0)
    natural = jnp.arange(head_size) ^ head_place

    def reordered(value):
        shape = value.shape
        return jnp.take(value.reshape(head_size, tok, shape[1]), natural, axis=0).reshape(shape)

    grad = reordered(dot_nn(cotangent, out_weight, short))
    grad_wide = grad.astype(wide)
    grad_start = (grad_wide * from_start).astype(short)
    local_adjoint = dot_tn(grad_start, state_output, short)
    adjoint = carried(local_adjoint, True)
    adjoint_short = adjoint.astype(short)

    product = dot_tn(cotangent, reordered(y_rounded), short)
    product = product.reshape(outer_seq, inner_seq, model_width // seq_size, inner_width)

    def picked(index):
        return lax.dynamic_index_in_dim(product, index, 1, False)

    mine = picked(inner_place).astype(wide)
    for m in range(1, inner_seq):
        mine = mine + flipped(picked(inner_place ^ m), "seq", m).astype(wide)
    mine_short = mine.astype(short)
    d_out = lax.dynamic_index_in_dim(mine, outer_place, 0, False)
    for m in range(1, outer_seq):
        piece = lax.dynamic_index_in_dim(mine_short, outer_place ^ m, 0, False)
        d_out = d_out + flipped(piece, "seq", m * inner_seq).astype(wide)
    d_out_weight = d_out.astype(short)

    dx_inner, later_sum, earlier_sum, db_inner, dc_inner = scan_backward(
        state_input, state_output, scan_input, grad, cumulative_t, cumulative
    )
    read_adjoint = dot_nt(state_input, adjoint_short) * to_end
    d_scan_input = (dx_inner + read_adjoint + skip_row * grad_wide).astype(short)
    input_part = db_inner + dot_nn(values_end, adjoint_short)
    output_part = dc_inner + dot_nn(grad_start, state_short)
    d_state_output = summed(output_part.astype(short), "head").astype(wide)
    d_state_input = summed(input_part.astype(short), "head").astype(wide)

    def head_sum(value):
        return jnp.dot(value, expand.T, precision=highest)

    d_skip_gain = summed(jnp.sum(head_sum(values * grad_wide), axis=0), "seq")
    growth = jnp.exp(total_decay)
    from_past = head_sum(read_state * grad_wide)
    to_future = head_sum(read_adjoint * values)
    corner = growth * jnp.sum(
        (state_in * adjoint).reshape(heads_local, head_dim * state_input.shape[1]), axis=1
    )
    forward_part = later_sum.T - earlier_sum + from_past
    d_log_decay = (
        lax.dot_general(
            lower_ones, forward_part, (((0,), (0,)), ((), ())),
            precision=highest, preferred_element_type=wide,
        )
        + jnp.dot(lower_ones - jnp.eye(seq_rows, dtype=wide), to_future, precision=highest)
        + corner[None, :]
    )
    return (
        d_hidden,
        d_norm_gain,
        d_route_weight,
        d_gate_weight,
        d_up_weight,
        d_down_weight,
        d_out_weight,
        d_scan_input,
        d_state_input,
        d_state_output,
        d_log_decay,
        d_skip_gain,
    )


def solution(mesh):
    in_specs = (
        P(("seq", "head"), None),
        P(),
        P(("seq", "head"), None),
        P(("seq", "head"), None),
        P(("seq", "head"), None, None),
        P(("seq", "head"), None, None),
        P(("seq", "head"), None, None),
        P(("seq", "head"), None),
        P("seq", "head"),
        P("seq", None),
        P("seq", None),
        P("seq", "head"),
        P("head"),
        P(None, "head"),
    )
    out_specs = (
        P(("seq", "head"), None),
        P(),
        P(("seq", "head"), None),
        P(("seq", "head"), None, None),
        P(("seq", "head"), None, None),
        P(("seq", "head"), None, None),
        P("seq", "head"),
        P("seq", "head"),
        P("seq", None),
        P("seq", None),
        P("seq", "head"),
        P("head"),
    )
    return jax.shard_map(shards, mesh=mesh, in_specs=in_specs, out_specs=out_specs, check_vma=False)
```

```python
import functools

import jax
import jax.numpy as jnp
from jax import lax
from jax.experimental import pallas as pl
from jax.experimental.pallas import tpu as pltpu
from jax.sharding import PartitionSpec as P

highest = lax.Precision.HIGHEST
epsilon = 1e-06
wide = jnp.float32
short = jnp.bfloat16
both = ("seq", "head")


def log2(number):
    return number.bit_length() - 1


def flipped(value, axis, mask):
    names = axis if isinstance(axis, tuple) else (axis,)
    size = 1
    for name in names:
        size = size * lax.axis_size(name)
    return lax.ppermute(value, axis, [(i, i ^ mask) for i in range(size)])


def shifted(value, axis, distance):
    size = lax.axis_size(axis)
    pairs = [(i, i + distance) for i in range(size) if 0 <= i + distance < size]
    return lax.ppermute(value, axis, pairs)


def summed(value, axis):
    size = lax.axis_size(axis)
    for bit in range(log2(size)):
        value = value + flipped(value, axis, 1 << bit)
    return value


light = pl.CostEstimate(flops=1, bytes_accessed=1, transcendentals=0)


def untouched(*refs):
    pass


def tied(value, *others):
    anywhere = pl.BlockSpec(memory_space=pl.ANY)
    return pl.pallas_call(
        untouched,
        out_shape=jax.ShapeDtypeStruct(value.shape, value.dtype),
        in_specs=[anywhere] * (1 + len(others)),
        out_specs=anywhere,
        input_output_aliases={0: 0},
        cost_estimate=light,
    )(value, *others)


def dot_nn(a, b, out=wide):
    return lax.dot_general(a, b, (((1,), (0,)), ((), ())), preferred_element_type=out)


def dot_nt(a, b, out=wide):
    return lax.dot_general(a, b, (((1,), (1,)), ((), ())), preferred_element_type=out)


def dot_tn(a, b, out=wide):
    return lax.dot_general(a, b, (((0,), (0,)), ((), ())), preferred_element_type=out)


def forward_kernel(heads, b_ref, c_ref, x_ref, row_ref, col_ref, y_ref, score_ref):
    step = pl.program_id(0)
    rows = b_ref.shape[0]

    @pl.when(step == 0)
    def _():
        score_ref[...] = dot_nt(c_ref[...], b_ref[...])

    scores = score_ref[...]
    keep = lax.broadcasted_iota(jnp.int32, (rows, rows), 0) >= lax.broadcasted_iota(
        jnp.int32, (rows, rows), 1
    )
    block = x_ref[...]
    width = block.shape[1]
    lane = lax.broadcasted_iota(jnp.int32, (rows, width), 1)
    head_lane = lax.broadcasted_iota(jnp.int32, col_ref.shape, 1)
    total = jnp.zeros((rows, width), wide)
    for k in range(heads):
        head = step * heads + k
        column = jnp.sum(jnp.where(head_lane == head, col_ref[...], 0.0), axis=1, keepdims=True)
        line = row_ref[pl.ds(head, 1), :]
        decay = jnp.where(keep, jnp.exp(jnp.minimum(column - line, 0.0)), 0.0)
        mine = (lane // (width // heads)) == k
        total = total + dot_nn(
            (decay * scores).astype(short), jnp.where(mine, block, jnp.zeros_like(block))
        )
    y_ref[...] = total


def backward_kernel(
    heads, b_ref, c_ref, x_ref, g_ref, row_ref, col_ref, *refs
):
    dx_ref, tsum_ref, ssum_ref, db_ref, dc_ref, score_ref, mask_ref = refs[-7:]
    step = pl.program_id(0)
    rows = b_ref.shape[0]

    @pl.when(step == 0)
    def _():
        score_ref[...] = dot_nt(b_ref[...], c_ref[...])
        mask_ref[...] = jnp.zeros_like(mask_ref)
        ssum_ref[...] = jnp.zeros_like(ssum_ref)

    scores = score_ref[...]
    keep = lax.broadcasted_iota(jnp.int32, (rows, rows), 0) <= lax.broadcasted_iota(
        jnp.int32, (rows, rows), 1
    )
    values = x_ref[...]
    grads = g_ref[...]
    width = values.shape[1]
    lane = lax.broadcasted_iota(jnp.int32, (rows, width), 1)
    head_lane = lax.broadcasted_iota(jnp.int32, col_ref.shape, 1)
    total = jnp.zeros((rows, width), wide)
    for k in range(heads):
        head = step * heads + k
        column = jnp.sum(jnp.where(head_lane == head, col_ref[...], 0.0), axis=1, keepdims=True)
        line = row_ref[pl.ds(head, 1), :]
        decay = jnp.where(keep, jnp.exp(jnp.minimum(line - column, 0.0)), 0.0)
        mine = (lane // (width // heads)) == k
        head_grads = jnp.where(mine, grads, jnp.zeros_like(grads))
        pair = decay * dot_nt(values, head_grads)
        mask_ref[...] += pair
        full = pair * scores
        tsum_ref[pl.ds(head, 1), :] = jnp.sum(full, axis=0, keepdims=True)
        ssum_ref[...] += jnp.where(head_lane == head, jnp.sum(full, axis=1, keepdims=True), 0.0)
        total = total + dot_nn((decay * scores).astype(short), head_grads)
    dx_ref[...] = total

    @pl.when(step == pl.num_programs(0) - 1)
    def _():
        mask = mask_ref[...].astype(short)
        db_ref[...] = dot_nn(mask, c_ref[...])
        dc_ref[...] = dot_tn(mask, b_ref[...])


inside = pl.BlockSpec(memory_space=pltpu.VMEM)
anywhere = pl.BlockSpec(memory_space=pl.ANY)
scalars = pl.BlockSpec(memory_space=pltpu.SMEM)
lanes = 128
mega = 1024 * 1024


def pack_kernel(count, cap, tok, experts, pick_ref, bundle_ref, *refs):
    outs, hit_ref = refs[-1 - count : -1], refs[-1]
    width = bundle_ref.shape[1]
    tail = bundle_ref[2 * tok :, :]
    table = [tail[:, i * tok : (i + 1) * tok] for i in range(2 * experts // 16)]
    table = jnp.concatenate(table, axis=0).astype(wide)
    line = lax.broadcasted_iota(jnp.int32, (experts, tok), 0)
    slot = lax.broadcasted_iota(jnp.int32, (cap, tok), 0).astype(wide)
    plain, scaled = [], []
    for k in range(count):
        mine = line == pick_ref[k]
        rank = jnp.sum(jnp.where(mine, table[:experts], 0.0), axis=0, keepdims=True)
        scale = jnp.sum(jnp.where(mine, table[experts:], 0.0), axis=0, keepdims=True)
        plain.append(jnp.where(rank == slot, 1.0, 0.0))
        scaled.append(jnp.where(rank == slot, scale, 0.0))
    plain = jnp.concatenate(plain, axis=0).astype(short)
    scaled = jnp.concatenate(scaled, axis=0).astype(short)
    hit_ref[...] = plain
    rows = dot_nn(plain, bundle_ref[:tok, :])
    grads = dot_nn(scaled, bundle_ref[tok : 2 * tok, :])
    for k in range(count):
        outs[k][:, :width] = rows[k * cap : (k + 1) * cap].astype(short)
        outs[k][:, width:] = grads[k * cap : (k + 1) * cap].astype(short)


def pack(pick, bundle, cap, tok, experts, ties):
    count, width = pick.shape[0], bundle.shape[1]
    out = pl.pallas_call(
        functools.partial(pack_kernel, count, cap, tok, experts),
        in_specs=[scalars, inside] + [anywhere] * len(ties),
        out_specs=[inside] * (count + 1),
        out_shape=[jax.ShapeDtypeStruct((cap, 2 * width), short)] * count
        + [jax.ShapeDtypeStruct((count * cap, tok), short)],
        compiler_params=pltpu.CompilerParams(vmem_limit_bytes=32 * mega),
        cost_estimate=light,
    )(pick, bundle, *ties)
    return list(out[:count]), out[count]


def expert_kernel(count, first, expert_ref, *refs):
    pieces, weights = refs[:count], refs[count : count + 4]
    outs = refs[-(count + 12) :]
    rows_out, outs = outs[:count], outs[count:]
    all_refs, (gu0, down0, gu1, down1), total_ref, sems = outs[:6], outs[6:10], outs[10], outs[11]
    copies = []
    for i, held in enumerate((gu0, down0, gu1, down1)):
        copies.append(pltpu.make_async_copy(weights[i], held, sems.at[i]))
        copies[i].start()
    cap = pieces[0].shape[0]
    width = pieces[0].shape[1] // 2
    half = down0.shape[0]
    both_rows = jnp.concatenate([piece[...].astype(wide) for piece in pieces], axis=0).astype(short)
    all_refs[0][...] = both_rows[:, :width]
    all_refs[1][...] = both_rows[:, width:]
    rows, grads = all_refs[0], all_refs[1]
    prob = jnp.zeros((rows.shape[0], 1), wide)
    for side in range(2):
        gate_up, down = ((gu0, down0), (gu1, down1))[side]
        copies[2 * side].wait()
        pre = dot_nn(rows[...], gate_up[...])
        copies[2 * side + 1].wait()
        back = dot_nt(grads[...], down[...])
        gate_pre, up_pre = pre[:, :half], pre[:, half:]
        sig = 1.0 / (1.0 + jnp.exp(-gate_pre))
        swish = gate_pre * sig
        active = (swish * up_pre).astype(short)
        prob = prob + jnp.sum(active.astype(wide) * back, axis=1, keepdims=True)
        all_refs[2 + side][...] = active
        d_pre = all_refs[4 + side]
        d_pre[:, :half] = (back * up_pre * sig * (1.0 + gate_pre * (1.0 - sig))).astype(short)
        d_pre[:, half:] = (back * swish).astype(short)
        term = dot_nt(d_pre[...], gate_up[...])
        if side == 0:
            total_ref[...] = term
        else:
            total_ref[...] += term
    lane = lax.broadcasted_iota(jnp.int32, (cap, lanes), 1)
    for k in range(count):
        span = slice(k * cap, (k + 1) * cap)
        rows_out[k][:, :width] = total_ref[span, :].astype(short)
        rows_out[k][:, width:] = jnp.where(lane == expert_ref[0], prob[span], 0.0).astype(short)


def expert_rows(expert, pieces, weights, index, blocks, kept, ties):
    count, cap = len(pieces), pieces[0].shape[0]
    width = pieces[0].shape[1] // 2
    rows = count * cap
    half = weights[0][1].shape[0]
    widths = (width, width, half, half, 2 * half, 2 * half)
    given = list(kept) if kept else []
    aliases = {1 + count + 4 + i: count + i for i in range(len(given))}
    out = pl.pallas_call(
        functools.partial(expert_kernel, count, not kept),
        grid=(1,),
        in_specs=[scalars]
        + [pl.BlockSpec((cap, 2 * width), lambda i: (0, 0))] * count
        + [anywhere] * (4 + len(given) + len(ties)),
        out_specs=[pl.BlockSpec((cap, width + lanes), lambda i: (0, 0))] * count
        + [pl.BlockSpec((rows, w), lambda i: (index, 0)) for w in widths],
        out_shape=[jax.ShapeDtypeStruct((cap, width + lanes), short)] * count
        + [jax.ShapeDtypeStruct((blocks * rows, w), short) for w in widths],
        scratch_shapes=[
            pltpu.VMEM((width, 2 * half), short),
            pltpu.VMEM((half, width), short),
            pltpu.VMEM((width, 2 * half), short),
            pltpu.VMEM((half, width), short),
            pltpu.VMEM((rows, width), wide),
            pltpu.SemaphoreType.DMA((4,)),
        ],
        input_output_aliases=aliases,
        compiler_params=pltpu.CompilerParams(vmem_limit_bytes=48 * mega),
        cost_estimate=light,
    )(expert, *pieces, *weights[0], *weights[1], *given, *ties)
    return out[:count], out[count:]


def weight_kernel(joined, rows_ref, grads_ref, act_ref, pre_ref, *refs):
    up = dot_tn(rows_ref[...], pre_ref[...])
    half = act_ref.shape[1]
    if joined:
        gate_out, up_out, down_out = refs[-3:]
        other = refs[0][...].astype(wide)
        up = up + other[:, : 2 * half]
        down = dot_tn(act_ref[...], grads_ref[...]) + other[:, 2 * half :].T
        gate_out[0] = up[:, :half].astype(short)
        up_out[0] = up[:, half:].astype(short)
        down_out[0] = down.astype(short)
    else:
        refs[-1][:, : 2 * half] = up.astype(short)
        refs[-1][:, 2 * half :] = dot_tn(grads_ref[...], act_ref[...]).astype(short)


def weight_terms(rows, grads, active, pre, others, ties):
    count, width = rows.shape
    half = active.shape[1]
    tile = min(256, width)
    column = pl.BlockSpec((count, tile), lambda i: (0, i))
    in_specs = [column, column]
    in_specs += [pl.BlockSpec(v.shape, lambda i: (0, 0)) for v in (active, pre)]
    term_spec = pl.BlockSpec((tile, 3 * half), lambda i: (i, 0))
    if others:
        in_specs.append(term_spec)
        out_specs = [pl.BlockSpec((1, tile, half), lambda i: (0, i, 0))] * 2
        out_specs.append(pl.BlockSpec((1, half, tile), lambda i: (0, 0, i)))
        out_shape = [(1, width, half), (1, width, half), (1, half, width)]
    else:
        out_specs = [term_spec]
        out_shape = [(width, 3 * half)]
    return pl.pallas_call(
        functools.partial(weight_kernel, bool(others)),
        grid=(width // tile,),
        in_specs=in_specs + [anywhere] * len(ties),
        out_specs=out_specs,
        out_shape=[jax.ShapeDtypeStruct(v, short) for v in out_shape],
        compiler_params=pltpu.CompilerParams(vmem_limit_bytes=40 * mega),
        cost_estimate=pl.CostEstimate(flops=4 * 10**9, bytes_accessed=1, transcendentals=0),
    )(rows, grads, active, pre, *others, *ties)


def scan_blocks(rows, state, width, heads_local):
    whole = pl.BlockSpec((rows, state), lambda i: (0, 0))
    column = pl.BlockSpec((rows, width), lambda i: (0, i))
    lines = pl.BlockSpec((heads_local, rows), lambda i: (0, 0))
    columns = pl.BlockSpec((rows, heads_local), lambda i: (0, 0))
    return whole, column, lines, columns


def scan_forward(b, c, x, lines, columns):
    rows, state = b.shape
    inner = x.shape[1]
    heads_local = columns.shape[1]
    width = 2 * (inner // heads_local)
    whole, column, line_spec, column_spec = scan_blocks(rows, state, width, heads_local)
    return pl.pallas_call(
        functools.partial(forward_kernel, 2),
        grid=(heads_local // 2,),
        in_specs=[whole, whole, column, line_spec, column_spec],
        out_specs=column,
        out_shape=jax.ShapeDtypeStruct((rows, inner), wide),
        scratch_shapes=[pltpu.VMEM((rows, rows), wide)],
        compiler_params=pltpu.CompilerParams(vmem_limit_bytes=24 * 1024 * 1024),
        cost_estimate=light,
    )(b, c, x, lines, columns)


def scan_backward(b, c, x, g, lines, columns, *ties):
    rows, state = b.shape
    inner = x.shape[1]
    heads_local = columns.shape[1]
    width = 2 * (inner // heads_local)
    whole, column, line_spec, column_spec = scan_blocks(rows, state, width, heads_local)
    return pl.pallas_call(
        functools.partial(backward_kernel, 2),
        grid=(heads_local // 2,),
        in_specs=[whole, whole, column, column, line_spec, column_spec]
        + [pl.BlockSpec(memory_space=pl.ANY)] * len(ties),
        out_specs=[column, line_spec, column_spec, whole, whole],
        out_shape=[
            jax.ShapeDtypeStruct((rows, inner), wide),
            jax.ShapeDtypeStruct((heads_local, rows), wide),
            jax.ShapeDtypeStruct((rows, heads_local), wide),
            jax.ShapeDtypeStruct((rows, state), wide),
            jax.ShapeDtypeStruct((rows, state), wide),
        ],
        scratch_shapes=[pltpu.VMEM((rows, rows), wide), pltpu.VMEM((rows, rows), wide)],
        compiler_params=pltpu.CompilerParams(vmem_limit_bytes=32 * 1024 * 1024),
        cost_estimate=pl.CostEstimate(flops=2 * 10**9, bytes_accessed=1, transcendentals=0),
    )(b, c, x, g, lines, columns, *ties)


def shards(
    hidden,
    norm_gain,
    expert_choice,
    route_weight,
    gate_weight,
    up_weight,
    down_weight,
    layer_grad,
    scan_input,
    state_input,
    state_output,
    log_decay,
    skip_gain,
    out_weight,
):
    seq_size, head_size = lax.axis_size("seq"), lax.axis_size("head")
    devices = seq_size * head_size
    experts = devices // 2
    tok, model_width = hidden.shape
    top_count = expert_choice.shape[1]
    cap = 9 * tok * top_count // (8 * experts)
    cap = (cap + 7) // 8 * 8
    groups = 1 << ((log2(devices)) // 2)
    plane = devices // groups
    plane_experts = plane // 2
    seq_place, head_place = lax.axis_index("seq"), lax.axis_index("head")
    place = seq_place * head_size + head_place
    group = place // plane

    def across(value, mask):
        return flipped(value, both, mask * plane)

    def spread(first):
        rows = [first]
        for m in range(1, groups):
            low = m & -m
            rows.append(across(rows[m ^ low], low))
        return rows

    chip = (place % plane) // 2

    def within(value, mask):
        return flipped(value, both, 2 * mask)

    seq_rows, inner_width = scan_input.shape
    heads_local = log_decay.shape[1]
    head_dim = inner_width // heads_local
    inner_seq = 1 << (log2(seq_size) // 2)
    outer_seq = seq_size // inner_seq
    inner_place, outer_place = seq_place % inner_seq, seq_place // inner_seq

    choice_t = expert_choice.T
    named = choice_t[None, :, :] == jnp.arange(experts, dtype=jnp.int32)[:, None, None]
    chosen = jnp.any(named, axis=1)
    before = jnp.arange(tok)[:, None] < jnp.arange(tok)[None, :]
    rank = dot_nn(chosen.astype(short), before.astype(short))
    rank = jnp.where(chosen, rank, -1.0).astype(short)
    route_t = route_weight.T.astype(wide)
    prob = jnp.sum(jnp.where(named, route_t[None], 0.0), axis=1).astype(short)
    tables = jnp.concatenate([rank, prob], axis=0)
    pieces = [tables[i : i + 16] for i in range(0, 2 * experts, 16)]
    pieces.append(jnp.zeros((16, model_width - tok * len(pieces)), short))
    table_rows = jnp.concatenate(pieces, axis=1)

    hidden_wide = hidden.astype(wide)
    inverse = lax.rsqrt(jnp.mean(hidden_wide * hidden_wide, axis=1, keepdims=True) + epsilon)
    normalized = hidden_wide * inverse
    normed = (normalized * norm_gain[None, :]).astype(short)
    bundles = spread(jnp.concatenate([normed, layer_grad, table_rows], axis=0))

    gate_up = jnp.concatenate([gate_weight[0], up_weight[0]], axis=1)

    order = jnp.arange(plane_experts, dtype=jnp.int32) ^ chip
    selected = group * plane_experts + order
    own_expert = selected[:1]

    hits, received, returning = [], [], []
    kept = None

    def dispatch(m):
        ties = []
        if m == 1:
            ties = [received[0][1]]
        elif m == 2:
            ties = [received[1][1]]
        elif m > 2:
            ties = [*received[m - 2], returning[m - 3][0]]
        sent, hit = pack(selected, bundles[m], cap, tok, experts, ties)
        hits.append(hit)
        pieces = [sent[0]]
        for k in range(1, plane_experts):
            outgoing = sent[k]
            if m == groups - 1 and k == plane_experts - 1:
                outgoing = tied(outgoing, returning[m - 2][0])
            pieces.append(within(outgoing, k))
        received.append(pieces)

    for m in range(min(3, groups)):
        dispatch(m)
    weights = [(gate_up, down_weight[0])]
    weights.append(
        (
            flipped(tied(gate_up, *received[0][1:]), "head", 1),
            flipped(tied(down_weight[0], *received[0][1:]), "head", 1),
        )
    )

    lower = jnp.arange(seq_rows)[:, None] >= jnp.arange(seq_rows)[None, :]
    lower_ones = lower.astype(wide)
    cumulative = jnp.dot(lower_ones, log_decay, precision=highest)
    cumulative_t = cumulative.T
    total_decay = cumulative[-1]
    head_of = (jnp.arange(inner_width) // head_dim)[None, :] == jnp.arange(heads_local)[:, None]
    expand = head_of.astype(wide)

    def expanded(value):
        return jnp.dot(value, expand, precision=highest)

    from_start = expanded(jnp.exp(cumulative))
    to_end = expanded(jnp.exp(total_decay[None, :] - cumulative))
    skip_row = expanded(skip_gain[None, :])
    values = scan_input.astype(wide)
    values_end = (values * to_end).astype(short)
    def columns_of(logs, valid):
        factors = jnp.exp(jnp.minimum(jnp.stack(logs, axis=0), 0.0))
        factors = jnp.where(jnp.stack([jnp.asarray(v) for v in valid])[:, None], factors, 0.0)
        return lax.dot_general(
            expand, factors, (((0,), (1,)), ((), ())), precision=highest,
            preferred_element_type=wide,
        )

    def combined(pieces, columns, first, step):
        total = jnp.zeros((inner_width, state_input.shape[1]), wide)
        for k, piece in enumerate(pieces):
            place_of = first + step * k
            total = total + columns[:, place_of : place_of + 1] * piece.astype(wide)
        return total

    def thirds(value, width):
        high = lax.reduce_precision(value, 8, 7)
        middle = lax.reduce_precision(value - high, 8, 7)
        rows = jnp.concatenate([high, middle, value - high - middle], axis=0)
        below = (rows.shape[0] + 15) // 16 * 16 - rows.shape[0]
        return jnp.pad(rows, ((0, below), (0, width - rows.shape[1]))).astype(short)

    def joined_thirds(rows, count, width):
        rows = rows[: 3 * count, :width].astype(wide)
        return rows[:count] + rows[count : 2 * count] + rows[2 * count :]

    start = outer_place * inner_seq
    local_state = tied(dot_tn(values_end, state_input, short), received[0][1])
    message = jnp.concatenate([local_state, thirds(total_decay[None, :], lanes)], axis=0)
    messages = [message] + [flipped(message, "seq", m) for m in range(1, inner_seq)]
    inner_totals = jnp.zeros((inner_seq, heads_local), wide)
    for m in range(inner_seq):
        piece = joined_thirds(messages[m][inner_width:], 1, heads_local)
        inner_totals = lax.dynamic_update_slice(inner_totals, piece, (inner_place ^ m, 0))
    inner_ended = jnp.concatenate(
        [jnp.zeros((1, heads_local), wide), jnp.cumsum(inner_totals, axis=0)], axis=0
    )

    def inner_before(index):
        return lax.dynamic_index_in_dim(inner_ended, index, 0, False)

    logs, valid = [], []
    for m in range(inner_seq):
        source = inner_place ^ m
        logs.append(inner_before(inner_place) - inner_before(source + 1))
        logs.append(inner_before(inner_seq) - inner_before(source + 1))
        valid.extend([source < inner_place, True])
    columns = columns_of(logs, valid)
    states = [v[:inner_width] for v in messages]
    state_in = combined(states, columns, 0, 2)
    for m in range(min(2, groups)):
        rows, kept = expert_rows(own_expert, received[m], weights, m, groups, kept, [])
        returning.append(rows)

    message = jnp.concatenate(
        [combined(states, columns, 1, 2).astype(short), thirds(inner_totals, lanes)], axis=0
    )
    message = tied(message, returning[-1][0])
    messages = [message] + [flipped(message, "seq", m * inner_seq) for m in range(1, outer_seq)]
    totals = jnp.zeros((seq_size, heads_local), wide)
    for m in range(outer_seq):
        piece = joined_thirds(messages[m][inner_width:], inner_seq, heads_local)
        totals = lax.dynamic_update_slice(totals, piece, ((outer_place ^ m) * inner_seq, 0))
    ended = jnp.concatenate(
        [jnp.zeros((1, heads_local), wide), jnp.cumsum(totals, axis=0)], axis=0
    )

    def before_of(index):
        return lax.dynamic_index_in_dim(ended, jnp.clip(index, 0, seq_size), 0, False)

    logs, valid = [], []
    for m in range(1, outer_seq):
        source = outer_place ^ m
        logs.append(before_of(seq_place) - before_of((source + 1) * inner_seq))
        valid.append(source < outer_place)
    columns = columns_of(logs, valid)
    state_in = state_in + combined([v[:inner_width] for v in messages[1:]], columns, 0, 1)

    logs, valid = [], []
    for m in range(inner_seq):
        source = start + (inner_place ^ m)
        logs.append(before_of(source) - before_of(seq_place + 1))
        logs.append(before_of(source) - before_of(start))
        valid.extend([source > seq_place, True])
    for k in range(1, outer_seq):
        logs.append(before_of(start + k * inner_seq) - before_of(seq_place + 1))
        valid.append(True)
    adjoint_columns = columns_of(logs, valid)

    state_short = state_in.astype(short)
    read_state = dot_nt(state_output, state_short) * from_start
    y_inner = scan_forward(state_input, state_output, scan_input, cumulative_t, cumulative)
    y_rounded = (y_inner + read_state + skip_row * values).astype(short)


    for m in range(2, groups):
        if m >= 3:
            dispatch(m)
        rows, kept = expert_rows(own_expert, received[m], weights, m, groups, kept, [])
        returning.append(rows)

    partial = [None] * groups
    for m in reversed(range(groups)):
        outgoing = list(returning[m])
        if m < groups - 1:
            after = partial[m + 2] if m < groups - 2 else returning[groups - 1][0]
            outgoing = outgoing[:1] + [tied(v, after) for v in outgoing[1:]]
        back = outgoing[:1] + [within(outgoing[k], k) for k in range(1, plane_experts)]
        partial[m] = dot_tn(hits[m], jnp.concatenate(back, axis=0))

    other_terms = weight_terms(kept[0], kept[1], kept[3], kept[5], (), [partial[0], y_rounded])[0]
    partial[0] = tied(partial[0], other_terms)

    bit = 1
    tree = {m: partial[m] for m in range(groups)}
    while bit < groups:
        moved = {m: across(tree[m].astype(short), bit) for m in tree if m & bit}
        tree = {m: tree[m] + moved[m ^ bit].astype(wide) for m in tree if not m & bit}
        bit = bit * 2
    d_normed = tree[0][:, :model_width]

    prob_tokens = tree[0][:, model_width : model_width + experts].T
    d_route = jnp.sum(jnp.where(named, prob_tokens[:, None, :], 0.0), axis=0)
    d_route_weight = (d_route / route_t).T.astype(short)

    gain_scaled = norm_gain[None, :] * d_normed
    centered = jnp.mean(gain_scaled * normalized, axis=1, keepdims=True)
    d_hidden = (
        layer_grad.astype(wide) + inverse * (gain_scaled - normalized * centered)
    ).astype(short)
    gain_part = jnp.sum(d_normed * normalized, axis=0)

    gain_rows = thirds(gain_part[None, :], model_width)
    blocks = {0: jnp.concatenate([d_hidden, gain_rows], axis=0)}
    for k in reversed(range(log2(head_size))):
        blocks.update({m ^ (1 << k): flipped(v, "head", 1 << k) for m, v in blocks.items()})
    cotangent = jnp.zeros((seq_rows, model_width), short)
    gains = jnp.zeros((head_size, model_width), wide)
    for m, value in blocks.items():
        spot = head_place ^ m
        cotangent = lax.dynamic_update_slice(cotangent, value[:tok], (spot * tok, 0))
        gains = lax.dynamic_update_slice(gains, joined_thirds(value[tok:], 1, model_width), (spot, 0))
    grad = dot_nn(cotangent, out_weight, short)
    grad_wide = grad.astype(wide)
    grad_start = (grad_wide * from_start).astype(short)
    local_adjoint = dot_tn(grad_start, state_output, short)

    block = model_width // seq_size
    chosen_cot = {}
    for m in range(inner_seq):
        columns = [
            lax.dynamic_slice(
                cotangent, (0, (o * inner_seq + (inner_place ^ m)) * block), (seq_rows, block)
            )
            for o in range(outer_seq)
        ]
        chosen_cot[m] = jnp.concatenate(columns, axis=1)
    adjoints = [local_adjoint] + [flipped(local_adjoint, "seq", m) for m in range(1, inner_seq)]
    adjoint = combined(adjoints, adjoint_columns, 0, 2)
    part_y = tied(y_rounded, local_adjoint)
    sent_products = [dot_tn(part_y, chosen_cot[m], short) for m in range(1, inner_seq)]
    moved = [flipped(v, "seq", m + 1) for m, v in enumerate(sent_products)]
    dx_inner, later_sum, earlier_sum, db_inner, dc_inner = scan_backward(
        state_input, state_output, scan_input, grad, cumulative_t, cumulative,
        sent_products[0],
    )
    adjoints[0] = tied(adjoints[0], dx_inner)
    joined = combined(adjoints, adjoint_columns, 1, 2).astype(short)
    later = [shifted(joined, "seq", -k * inner_seq) for k in range(1, outer_seq)]
    other_terms = flipped(tied(other_terms, cotangent), "head", 1)
    product = dot_tn(tied(part_y, joined), chosen_cot[0])
    for value in moved:
        product = product + value.astype(wide)
    adjoint = adjoint + combined(later, adjoint_columns, 2 * inner_seq, 1)
    adjoint_short = adjoint.astype(short)
    product_short = product.astype(short)
    moved = []
    for m in range(1, outer_seq):
        piece = lax.dynamic_slice(
            product_short, (0, (outer_place ^ m) * block), (inner_width, block)
        )
        moved.append(flipped(piece, "seq", m * inner_seq))

    read_adjoint = dot_nt(state_input, adjoint_short) * to_end
    d_scan_input = (dx_inner + read_adjoint + skip_row * grad_wide).astype(short)
    input_part = db_inner + dot_nn(values_end, adjoint_short)
    output_part = dc_inner + dot_nn(grad_start, state_short)
    shared = jnp.concatenate([input_part, output_part], axis=0).astype(short)
    d_gate_weight, d_up_weight, d_down_weight = weight_terms(
        kept[0], kept[1], kept[2], kept[4], (other_terms,), [shared]
    )
    for k in range(log2(head_size)):
        other = flipped(shared, "head", 1 << k)
        if k == log2(head_size) - 1:
            shared = tied(shared, d_down_weight)
        shared = shared + other
    shared = shared.astype(wide)
    d_out = lax.dynamic_slice(product, (0, outer_place * block), (inner_width, block))
    d_out = tied(d_out, d_down_weight)
    for value in moved:
        d_out = d_out + value.astype(wide)
    d_out_weight = d_out.T.astype(short)
    d_state_input, d_state_output = shared[:seq_rows], shared[seq_rows:]

    def head_sum(value):
        return jnp.dot(value, expand.T, precision=highest)

    skip_part = jnp.sum(head_sum(values * grad_wide), axis=0)
    skip_part = jnp.pad(skip_part, (0, lanes - heads_local))
    tail_sum = jnp.concatenate([jnp.sum(gains, axis=0), skip_part], axis=0)
    tail_sum = summed(tied(tail_sum, adjoint_short), "seq")
    d_norm_gain = tail_sum[:model_width]
    d_skip_gain = tail_sum[model_width : model_width + heads_local]
    growth = jnp.exp(total_decay)
    from_past = head_sum(read_state * grad_wide)
    to_future = head_sum(read_adjoint * values)
    corner = growth * jnp.sum(
        (state_in * adjoint).reshape(heads_local, head_dim * state_input.shape[1]), axis=1
    )
    forward_part = later_sum.T - earlier_sum + from_past
    d_log_decay = (
        lax.dot_general(
            lower_ones, forward_part, (((0,), (0,)), ((), ())),
            precision=highest, preferred_element_type=wide,
        )
        + jnp.dot(lower_ones - jnp.eye(seq_rows, dtype=wide), to_future, precision=highest)
        + corner[None, :]
    )
    return (
        d_hidden,
        d_norm_gain,
        d_route_weight,
        d_gate_weight,
        d_up_weight,
        d_down_weight,
        d_out_weight,
        d_scan_input,
        d_state_input,
        d_state_output,
        d_log_decay,
        d_skip_gain,
    )


def solution(mesh):
    in_specs = (
        P(("seq", "head"), None),
        P(),
        P(("seq", "head"), None),
        P(("seq", "head"), None),
        P(("seq", "head"), None, None),
        P(("seq", "head"), None, None),
        P(("seq", "head"), None, None),
        P(("seq", "head"), None),
        P("seq", "head"),
        P("seq", None),
        P("seq", None),
        P("seq", "head"),
        P("head"),
        P(None, "head"),
    )
    out_specs = (
        P(("seq", "head"), None),
        P(),
        P(("seq", "head"), None),
        P(("seq", "head"), None, None),
        P(("seq", "head"), None, None),
        P(("seq", "head"), None, None),
        P("seq", "head"),
        P("seq", "head"),
        P("seq", None),
        P("seq", None),
        P("seq", "head"),
        P("head"),
    )
    return jax.shard_map(shards, mesh=mesh, in_specs=in_specs, out_specs=out_specs, check_vma=False)
```

```python
import functools

import jax
import jax.numpy as jnp
from jax import lax
from jax.experimental import pallas as pl
from jax.experimental.pallas import tpu as pltpu
from jax.sharding import PartitionSpec as P

highest = lax.Precision.HIGHEST
epsilon = 1e-06
wide = jnp.float32
short = jnp.bfloat16
both = ("seq", "head")


def log2(number):
    return number.bit_length() - 1


def flipped(value, axis, mask):
    names = axis if isinstance(axis, tuple) else (axis,)
    size = 1
    for name in names:
        size = size * lax.axis_size(name)
    return lax.ppermute(value, axis, [(i, i ^ mask) for i in range(size)])


def shifted(value, axis, distance):
    size = lax.axis_size(axis)
    pairs = [(i, i + distance) for i in range(size) if 0 <= i + distance < size]
    return lax.ppermute(value, axis, pairs)


def summed(value, axis):
    size = lax.axis_size(axis)
    for bit in range(log2(size)):
        value = value + flipped(value, axis, 1 << bit)
    return value


light = pl.CostEstimate(flops=1, bytes_accessed=1, transcendentals=0)


def untouched(*refs):
    pass


def tied(value, *others):
    anywhere = pl.BlockSpec(memory_space=pl.ANY)
    return pl.pallas_call(
        untouched,
        out_shape=jax.ShapeDtypeStruct(value.shape, value.dtype),
        in_specs=[anywhere] * (1 + len(others)),
        out_specs=anywhere,
        input_output_aliases={0: 0},
        cost_estimate=light,
    )(value, *others)


def dot_nn(a, b, out=wide):
    return lax.dot_general(a, b, (((1,), (0,)), ((), ())), preferred_element_type=out)


def dot_nt(a, b, out=wide):
    return lax.dot_general(a, b, (((1,), (1,)), ((), ())), preferred_element_type=out)


def dot_tn(a, b, out=wide):
    return lax.dot_general(a, b, (((0,), (0,)), ((), ())), preferred_element_type=out)


def forward_kernel(heads, b_ref, c_ref, x_ref, row_ref, col_ref, y_ref, score_ref):
    step = pl.program_id(0)
    rows = b_ref.shape[0]

    @pl.when(step == 0)
    def _():
        score_ref[...] = dot_nt(c_ref[...], b_ref[...])

    scores = score_ref[...]
    keep = lax.broadcasted_iota(jnp.int32, (rows, rows), 0) >= lax.broadcasted_iota(
        jnp.int32, (rows, rows), 1
    )
    block = x_ref[...]
    width = block.shape[1]
    lane = lax.broadcasted_iota(jnp.int32, (rows, width), 1)
    head_lane = lax.broadcasted_iota(jnp.int32, col_ref.shape, 1)
    total = jnp.zeros((rows, width), wide)
    for k in range(heads):
        head = step * heads + k
        column = jnp.sum(jnp.where(head_lane == head, col_ref[...], 0.0), axis=1, keepdims=True)
        line = row_ref[pl.ds(head, 1), :]
        decay = jnp.where(keep, jnp.exp(jnp.minimum(column - line, 0.0)), 0.0)
        mine = (lane // (width // heads)) == k
        total = total + dot_nn(
            (decay * scores).astype(short), jnp.where(mine, block, jnp.zeros_like(block))
        )
    y_ref[...] = total


def backward_kernel(
    heads, b_ref, c_ref, x_ref, g_ref, row_ref, col_ref, *refs
):
    dx_ref, tsum_ref, ssum_ref, db_ref, dc_ref, score_ref, mask_ref = refs[-7:]
    step = pl.program_id(0)
    rows = b_ref.shape[0]

    @pl.when(step == 0)
    def _():
        score_ref[...] = dot_nt(b_ref[...], c_ref[...])
        mask_ref[...] = jnp.zeros_like(mask_ref)
        ssum_ref[...] = jnp.zeros_like(ssum_ref)

    scores = score_ref[...]
    keep = lax.broadcasted_iota(jnp.int32, (rows, rows), 0) <= lax.broadcasted_iota(
        jnp.int32, (rows, rows), 1
    )
    values = x_ref[...]
    grads = g_ref[...]
    width = values.shape[1]
    lane = lax.broadcasted_iota(jnp.int32, (rows, width), 1)
    head_lane = lax.broadcasted_iota(jnp.int32, col_ref.shape, 1)
    total = jnp.zeros((rows, width), wide)
    for k in range(heads):
        head = step * heads + k
        column = jnp.sum(jnp.where(head_lane == head, col_ref[...], 0.0), axis=1, keepdims=True)
        line = row_ref[pl.ds(head, 1), :]
        decay = jnp.where(keep, jnp.exp(jnp.minimum(line - column, 0.0)), 0.0)
        mine = (lane // (width // heads)) == k
        head_grads = jnp.where(mine, grads, jnp.zeros_like(grads))
        pair = decay * dot_nt(values, head_grads)
        mask_ref[...] += pair
        full = pair * scores
        tsum_ref[pl.ds(head, 1), :] = jnp.sum(full, axis=0, keepdims=True)
        ssum_ref[...] += jnp.where(head_lane == head, jnp.sum(full, axis=1, keepdims=True), 0.0)
        total = total + dot_nn((decay * scores).astype(short), head_grads)
    dx_ref[...] = total

    @pl.when(step == pl.num_programs(0) - 1)
    def _():
        mask = mask_ref[...].astype(short)
        db_ref[...] = dot_nn(mask, c_ref[...])
        dc_ref[...] = dot_tn(mask, b_ref[...])


inside = pl.BlockSpec(memory_space=pltpu.VMEM)
anywhere = pl.BlockSpec(memory_space=pl.ANY)
scalars = pl.BlockSpec(memory_space=pltpu.SMEM)
lanes = 128
mega = 1024 * 1024


def pack_kernel(count, cap, tok, experts, pick_ref, bundle_ref, *refs):
    outs, hit_ref = refs[-1 - count : -1], refs[-1]
    width = bundle_ref.shape[1]
    tail = bundle_ref[2 * tok :, :]
    table = [tail[:, i * tok : (i + 1) * tok] for i in range(2 * experts // 16)]
    table = jnp.concatenate(table, axis=0).astype(wide)
    line = lax.broadcasted_iota(jnp.int32, (experts, tok), 0)
    slot = lax.broadcasted_iota(jnp.int32, (cap, tok), 0).astype(wide)
    plain, scaled = [], []
    for k in range(count):
        mine = line == pick_ref[k]
        rank = jnp.sum(jnp.where(mine, table[:experts], 0.0), axis=0, keepdims=True)
        scale = jnp.sum(jnp.where(mine, table[experts:], 0.0), axis=0, keepdims=True)
        plain.append(jnp.where(rank == slot, 1.0, 0.0))
        scaled.append(jnp.where(rank == slot, scale, 0.0))
    plain = jnp.concatenate(plain, axis=0).astype(short)
    scaled = jnp.concatenate(scaled, axis=0).astype(short)
    hit_ref[...] = plain
    rows = dot_nn(plain, bundle_ref[:tok, :])
    grads = dot_nn(scaled, bundle_ref[tok : 2 * tok, :])
    for k in range(count):
        outs[k][:, :width] = rows[k * cap : (k + 1) * cap].astype(short)
        outs[k][:, width:] = grads[k * cap : (k + 1) * cap].astype(short)


def pack(pick, bundle, cap, tok, experts, ties):
    count, width = pick.shape[0], bundle.shape[1]
    out = pl.pallas_call(
        functools.partial(pack_kernel, count, cap, tok, experts),
        in_specs=[scalars, inside] + [anywhere] * len(ties),
        out_specs=[inside] * (count + 1),
        out_shape=[jax.ShapeDtypeStruct((cap, 2 * width), short)] * count
        + [jax.ShapeDtypeStruct((count * cap, tok), short)],
        compiler_params=pltpu.CompilerParams(vmem_limit_bytes=32 * mega),
        cost_estimate=light,
    )(pick, bundle, *ties)
    return list(out[:count]), out[count]


def expert_kernel(count, first, expert_ref, *refs):
    pieces, weights = refs[:count], refs[count : count + 4]
    outs = refs[-(count + 9) :]
    rows_out, outs = outs[:count], outs[count:]
    all_refs, (gu0, down0, gu1, down1), total_ref, sems = outs[:3], outs[3:7], outs[7], outs[8]
    copies = []
    for i, held in enumerate((gu0, down0, gu1, down1)):
        copies.append(pltpu.make_async_copy(weights[i], held, sems.at[i]))
        copies[i].start()
    cap = pieces[0].shape[0]
    width = pieces[0].shape[1] // 2
    half = down0.shape[0]
    both_rows = jnp.concatenate([piece[...].astype(wide) for piece in pieces], axis=0).astype(short)
    all_refs[0][...] = both_rows[:, :width]
    all_refs[1][...] = both_rows[:, width:]
    rows, grads = all_refs[0], all_refs[1]
    prob = jnp.zeros((rows.shape[0], 1), wide)
    for side in range(2):
        gate_up, down = ((gu0, down0), (gu1, down1))[side]
        copies[2 * side].wait()
        pre = dot_nn(rows[...], gate_up[...])
        copies[2 * side + 1].wait()
        back = dot_nt(grads[...], down[...])
        gate_pre, up_pre = pre[:, :half], pre[:, half:]
        sig = 1.0 / (1.0 + jnp.exp(-gate_pre))
        swish = gate_pre * sig
        active = (swish * up_pre).astype(short)
        prob = prob + jnp.sum(active.astype(wide) * back, axis=1, keepdims=True)
        held = all_refs[2]
        low = 2 * half * (1 + side)
        held[:, side * half : (side + 1) * half] = active
        d_gate = back * up_pre * sig * (1.0 + gate_pre * (1.0 - sig))
        held[:, low : low + half] = d_gate.astype(short)
        held[:, low + half : low + 2 * half] = (back * swish).astype(short)
        term = dot_nt(held[:, low : low + 2 * half], gate_up[...])
        if side == 0:
            total_ref[...] = term
        else:
            total_ref[...] += term
    lane = lax.broadcasted_iota(jnp.int32, (cap, lanes), 1)
    for k in range(count):
        span = slice(k * cap, (k + 1) * cap)
        rows_out[k][:, :width] = total_ref[span, :].astype(short)
        rows_out[k][:, width:] = jnp.where(lane == expert_ref[0], prob[span], 0.0).astype(short)


def expert_rows(expert, pieces, weights, index, blocks, kept, ties):
    count, cap = len(pieces), pieces[0].shape[0]
    width = pieces[0].shape[1] // 2
    rows = count * cap
    half = weights[0][1].shape[0]
    widths = (width, width, 6 * half)
    given = list(kept) if kept else []
    aliases = {1 + count + 4 + i: count + i for i in range(len(given))}
    out = pl.pallas_call(
        functools.partial(expert_kernel, count, not kept),
        grid=(1,),
        in_specs=[scalars]
        + [pl.BlockSpec((cap, 2 * width), lambda i: (0, 0))] * count
        + [anywhere] * (4 + len(given) + len(ties)),
        out_specs=[pl.BlockSpec((cap, width + lanes), lambda i: (0, 0))] * count
        + [pl.BlockSpec((rows, w), lambda i: (index, 0)) for w in widths],
        out_shape=[jax.ShapeDtypeStruct((cap, width + lanes), short)] * count
        + [jax.ShapeDtypeStruct((blocks * rows, w), short) for w in widths],
        scratch_shapes=[
            pltpu.VMEM((width, 2 * half), short),
            pltpu.VMEM((half, width), short),
            pltpu.VMEM((width, 2 * half), short),
            pltpu.VMEM((half, width), short),
            pltpu.VMEM((rows, width), wide),
            pltpu.SemaphoreType.DMA((4,)),
        ],
        input_output_aliases=aliases,
        compiler_params=pltpu.CompilerParams(vmem_limit_bytes=48 * mega),
        cost_estimate=light,
    )(expert, *pieces, *weights[0], *weights[1], *given, *ties)
    return out[:count], out[count:]


def weight_kernel(joined, rows_ref, grads_ref, act_ref, pre_ref, *refs):
    up = dot_tn(rows_ref[...], pre_ref[...])
    half = act_ref.shape[1]
    if joined:
        gate_out, up_out, down_out = refs[-3:]
        other = refs[0][...].astype(wide)
        up = up + other[:, : 2 * half]
        down = dot_tn(act_ref[...], grads_ref[...]) + other[:, 2 * half :].T
        gate_out[0] = up[:, :half].astype(short)
        up_out[0] = up[:, half:].astype(short)
        down_out[0] = down.astype(short)
    else:
        refs[-1][:, : 2 * half] = up.astype(short)
        refs[-1][:, 2 * half :] = dot_tn(grads_ref[...], act_ref[...]).astype(short)


def weight_terms(rows, grads, held, side, others, ties):
    count, width = rows.shape
    half = held.shape[1] // 6
    tile = min(256, width)
    column = pl.BlockSpec((count, tile), lambda i: (0, i))
    in_specs = [column, column]
    in_specs.append(pl.BlockSpec((count, half), lambda i: (0, side)))
    in_specs.append(pl.BlockSpec((count, 2 * half), lambda i: (0, 1 + side)))
    term_spec = pl.BlockSpec((tile, 3 * half), lambda i: (i, 0))
    if others:
        in_specs.append(term_spec)
        out_specs = [pl.BlockSpec((1, tile, half), lambda i: (0, i, 0))] * 2
        out_specs.append(pl.BlockSpec((1, half, tile), lambda i: (0, 0, i)))
        out_shape = [(1, width, half), (1, width, half), (1, half, width)]
    else:
        out_specs = [term_spec]
        out_shape = [(width, 3 * half)]
    return pl.pallas_call(
        functools.partial(weight_kernel, bool(others)),
        grid=(width // tile,),
        in_specs=in_specs + [anywhere] * len(ties),
        out_specs=out_specs,
        out_shape=[jax.ShapeDtypeStruct(v, short) for v in out_shape],
        compiler_params=pltpu.CompilerParams(vmem_limit_bytes=40 * mega),
        cost_estimate=light,
    )(rows, grads, held, held, *others, *ties)


def scan_blocks(rows, state, width, heads_local):
    whole = pl.BlockSpec((rows, state), lambda i: (0, 0))
    column = pl.BlockSpec((rows, width), lambda i: (0, i))
    lines = pl.BlockSpec((heads_local, rows), lambda i: (0, 0))
    columns = pl.BlockSpec((rows, heads_local), lambda i: (0, 0))
    return whole, column, lines, columns


def scan_forward(b, c, x, lines, columns):
    rows, state = b.shape
    inner = x.shape[1]
    heads_local = columns.shape[1]
    width = 2 * (inner // heads_local)
    whole, column, line_spec, column_spec = scan_blocks(rows, state, width, heads_local)
    return pl.pallas_call(
        functools.partial(forward_kernel, 2),
        grid=(heads_local // 2,),
        in_specs=[whole, whole, column, line_spec, column_spec],
        out_specs=column,
        out_shape=jax.ShapeDtypeStruct((rows, inner), wide),
        scratch_shapes=[pltpu.VMEM((rows, rows), wide)],
        compiler_params=pltpu.CompilerParams(vmem_limit_bytes=24 * 1024 * 1024),
        cost_estimate=light,
    )(b, c, x, lines, columns)


def scan_backward(b, c, x, g, lines, columns, *ties):
    rows, state = b.shape
    inner = x.shape[1]
    heads_local = columns.shape[1]
    width = 2 * (inner // heads_local)
    whole, column, line_spec, column_spec = scan_blocks(rows, state, width, heads_local)
    return pl.pallas_call(
        functools.partial(backward_kernel, 2),
        grid=(heads_local // 2,),
        in_specs=[whole, whole, column, column, line_spec, column_spec]
        + [pl.BlockSpec(memory_space=pl.ANY)] * len(ties),
        out_specs=[column, line_spec, column_spec, whole, whole],
        out_shape=[
            jax.ShapeDtypeStruct((rows, inner), wide),
            jax.ShapeDtypeStruct((heads_local, rows), wide),
            jax.ShapeDtypeStruct((rows, heads_local), wide),
            jax.ShapeDtypeStruct((rows, state), wide),
            jax.ShapeDtypeStruct((rows, state), wide),
        ],
        scratch_shapes=[pltpu.VMEM((rows, rows), wide), pltpu.VMEM((rows, rows), wide)],
        compiler_params=pltpu.CompilerParams(vmem_limit_bytes=32 * 1024 * 1024),
        cost_estimate=pl.CostEstimate(flops=2 * 10**9, bytes_accessed=1, transcendentals=0),
    )(b, c, x, g, lines, columns, *ties)


def shards(
    hidden,
    norm_gain,
    expert_choice,
    route_weight,
    gate_weight,
    up_weight,
    down_weight,
    layer_grad,
    scan_input,
    state_input,
    state_output,
    log_decay,
    skip_gain,
    out_weight,
):
    seq_size, head_size = lax.axis_size("seq"), lax.axis_size("head")
    devices = seq_size * head_size
    experts = devices // 2
    tok, model_width = hidden.shape
    top_count = expert_choice.shape[1]
    cap = 9 * tok * top_count // (8 * experts)
    cap = (cap + 7) // 8 * 8
    groups = 1 << ((log2(devices)) // 2)
    plane = devices // groups
    plane_experts = plane // 2
    seq_place, head_place = lax.axis_index("seq"), lax.axis_index("head")
    place = seq_place * head_size + head_place
    group = place // plane

    def across(value, mask):
        return flipped(value, both, mask * plane)

    def spread(first):
        rows = [first]
        for m in range(1, groups):
            low = m & -m
            rows.append(across(rows[m ^ low], low))
        return rows

    chip = (place % plane) // 2

    def within(value, mask):
        return flipped(value, both, 2 * mask)

    seq_rows, inner_width = scan_input.shape
    heads_local = log_decay.shape[1]
    head_dim = inner_width // heads_local
    inner_seq = 1 << (log2(seq_size) // 2)
    outer_seq = seq_size // inner_seq
    inner_place, outer_place = seq_place % inner_seq, seq_place // inner_seq

    choice_t = expert_choice.T
    named = choice_t[None, :, :] == jnp.arange(experts, dtype=jnp.int32)[:, None, None]
    chosen = jnp.any(named, axis=1)
    before = jnp.arange(tok)[:, None] < jnp.arange(tok)[None, :]
    rank = dot_nn(chosen.astype(short), before.astype(short))
    rank = jnp.where(chosen, rank, -1.0).astype(short)
    route_t = route_weight.T.astype(wide)
    prob = jnp.sum(jnp.where(named, route_t[None], 0.0), axis=1).astype(short)
    tables = jnp.concatenate([rank, prob], axis=0)
    pieces = [tables[i : i + 16] for i in range(0, 2 * experts, 16)]
    pieces.append(jnp.zeros((16, model_width - tok * len(pieces)), short))
    table_rows = jnp.concatenate(pieces, axis=1)

    hidden_wide = hidden.astype(wide)
    inverse = lax.rsqrt(jnp.mean(hidden_wide * hidden_wide, axis=1, keepdims=True) + epsilon)
    normalized = hidden_wide * inverse
    normed = (normalized * norm_gain[None, :]).astype(short)
    bundles = spread(jnp.concatenate([normed, layer_grad, table_rows], axis=0))

    gate_up = jnp.concatenate([gate_weight[0], up_weight[0]], axis=1)

    order = jnp.arange(plane_experts, dtype=jnp.int32) ^ chip
    selected = group * plane_experts + order
    own_expert = selected[:1]

    hits, received, returning = [], [], []
    kept = None

    packed = []

    def prepare(m):
        ties = []
        if m == 1:
            ties = [received[0][1]]
        elif m == 2:
            ties = [received[1][1]]
        elif m > 2:
            ties = [*received[m - 2], returning[m - 3][0]]
        sent, hit = pack(selected, bundles[m], cap, tok, experts, ties)
        hits.append(hit)
        packed.append(sent)

    def send(m):
        pieces = [packed[m][0]]
        for k in range(1, plane_experts):
            outgoing = packed[m][k]
            if m == groups - 1 and k == plane_experts - 1:
                outgoing = tied(outgoing, returning[m - 2][0])
            pieces.append(within(outgoing, k))
        received.append(pieces)

    def work(m, kept):
        ties = [hits[m + 2]] if 1 <= m < groups - 2 else []
        rows, kept = expert_rows(own_expert, received[m], weights, m, groups, kept, ties)
        returning.append(rows)
        return kept

    for m in range(min(3, groups)):
        prepare(m)
        send(m)
    weights = [(gate_up, down_weight[0])]
    weights.append(
        (
            flipped(tied(gate_up, *received[0][1:]), "head", 1),
            flipped(tied(down_weight[0], *received[0][1:]), "head", 1),
        )
    )

    lower = jnp.arange(seq_rows)[:, None] >= jnp.arange(seq_rows)[None, :]
    lower_ones = lower.astype(wide)
    cumulative = jnp.dot(lower_ones, log_decay, precision=highest)
    cumulative_t = cumulative.T
    total_decay = cumulative[-1]
    head_of = (jnp.arange(inner_width) // head_dim)[None, :] == jnp.arange(heads_local)[:, None]
    expand = head_of.astype(wide)

    def expanded(value):
        return jnp.dot(value, expand, precision=highest)

    from_start = expanded(jnp.exp(cumulative))
    to_end = expanded(jnp.exp(total_decay[None, :] - cumulative))
    skip_row = expanded(skip_gain[None, :])
    values = scan_input.astype(wide)
    values_end = (values * to_end).astype(short)
    def columns_of(logs, valid):
        factors = jnp.exp(jnp.minimum(jnp.stack(logs, axis=0), 0.0))
        factors = jnp.where(jnp.stack([jnp.asarray(v) for v in valid])[:, None], factors, 0.0)
        return lax.dot_general(
            expand, factors, (((0,), (1,)), ((), ())), precision=highest,
            preferred_element_type=wide,
        )

    def combined(pieces, columns, first, step):
        total = jnp.zeros((inner_width, state_input.shape[1]), wide)
        for k, piece in enumerate(pieces):
            place_of = first + step * k
            total = total + columns[:, place_of : place_of + 1] * piece.astype(wide)
        return total

    def thirds(value, width):
        high = lax.reduce_precision(value, 8, 7)
        middle = lax.reduce_precision(value - high, 8, 7)
        rows = jnp.concatenate([high, middle, value - high - middle], axis=0)
        below = (rows.shape[0] + 15) // 16 * 16 - rows.shape[0]
        return jnp.pad(rows, ((0, below), (0, width - rows.shape[1]))).astype(short)

    def joined_thirds(rows, count, width):
        rows = rows[: 3 * count, :width].astype(wide)
        return rows[:count] + rows[count : 2 * count] + rows[2 * count :]

    start = outer_place * inner_seq
    local_state = tied(dot_tn(values_end, state_input, short), received[0][1])
    message = jnp.concatenate([local_state, thirds(total_decay[None, :], lanes)], axis=0)
    messages = [message] + [flipped(message, "seq", m) for m in range(1, inner_seq)]
    inner_totals = jnp.zeros((inner_seq, heads_local), wide)
    for m in range(inner_seq):
        piece = joined_thirds(messages[m][inner_width:], 1, heads_local)
        inner_totals = lax.dynamic_update_slice(inner_totals, piece, (inner_place ^ m, 0))
    inner_ended = jnp.concatenate(
        [jnp.zeros((1, heads_local), wide), jnp.cumsum(inner_totals, axis=0)], axis=0
    )

    def inner_before(index):
        return lax.dynamic_index_in_dim(inner_ended, index, 0, False)

    logs, valid = [], []
    for m in range(inner_seq):
        source = inner_place ^ m
        logs.append(inner_before(inner_place) - inner_before(source + 1))
        logs.append(inner_before(inner_seq) - inner_before(source + 1))
        valid.extend([source < inner_place, True])
    columns = columns_of(logs, valid)
    states = [v[:inner_width] for v in messages]
    state_in = combined(states, columns, 0, 2)
    for m in range(min(2, groups)):
        if 3 <= m + 2 < groups:
            prepare(m + 2)
        kept = work(m, kept)
        if 3 <= m + 2 < groups:
            send(m + 2)

    message = jnp.concatenate(
        [combined(states, columns, 1, 2).astype(short), thirds(inner_totals, lanes)], axis=0
    )
    message = tied(message, received[-1][1])
    messages = [message] + [flipped(message, "seq", m * inner_seq) for m in range(1, outer_seq)]
    totals = jnp.zeros((seq_size, heads_local), wide)
    for m in range(outer_seq):
        piece = joined_thirds(messages[m][inner_width:], inner_seq, heads_local)
        totals = lax.dynamic_update_slice(totals, piece, ((outer_place ^ m) * inner_seq, 0))
    ended = jnp.concatenate(
        [jnp.zeros((1, heads_local), wide), jnp.cumsum(totals, axis=0)], axis=0
    )

    def before_of(index):
        return lax.dynamic_index_in_dim(ended, jnp.clip(index, 0, seq_size), 0, False)

    logs, valid = [], []
    for m in range(1, outer_seq):
        source = outer_place ^ m
        logs.append(before_of(seq_place) - before_of((source + 1) * inner_seq))
        valid.append(source < outer_place)
    columns = columns_of(logs, valid)
    state_in = state_in + combined([v[:inner_width] for v in messages[1:]], columns, 0, 1)

    logs, valid = [], []
    for m in range(inner_seq):
        source = start + (inner_place ^ m)
        logs.append(before_of(source) - before_of(seq_place + 1))
        logs.append(before_of(source) - before_of(start))
        valid.extend([source > seq_place, True])
    for k in range(1, outer_seq):
        logs.append(before_of(start + k * inner_seq) - before_of(seq_place + 1))
        valid.append(True)
    adjoint_columns = columns_of(logs, valid)

    state_short = state_in.astype(short)
    read_state = dot_nt(state_output, state_short) * from_start
    y_inner = scan_forward(state_input, state_output, scan_input, cumulative_t, cumulative)
    y_rounded = (y_inner + read_state + skip_row * values).astype(short)


    for m in range(2, groups):
        if m + 2 < groups:
            prepare(m + 2)
        kept = work(m, kept)
        if m + 2 < groups:
            send(m + 2)

    partial = [None] * groups
    for m in reversed(range(groups)):
        outgoing = list(returning[m])
        if m < groups - 1:
            after = partial[m + 2] if m < groups - 2 else returning[groups - 1][0]
            outgoing = outgoing[:1] + [tied(v, after) for v in outgoing[1:]]
        back = outgoing[:1] + [within(outgoing[k], k) for k in range(1, plane_experts)]
        partial[m] = dot_tn(hits[m], jnp.concatenate(back, axis=0))

    def sorted_blocks(value):
        width = value.shape[1]
        return jnp.concatenate(
            [
                lax.dynamic_slice(value, ((head_place ^ n) * tok, 0), (tok, width))
                for n in range(head_size)
            ],
            axis=0,
        )

    y_sorted = sorted_blocks(y_rounded)

    other_terms = weight_terms(*kept, 1, (), [partial[0], y_sorted])[0]
    partial[0] = tied(partial[0], other_terms)

    bit = 1
    tree = {m: partial[m] for m in range(groups)}
    while bit < groups:
        moved = {m: across(tree[m].astype(short), bit) for m in tree if m & bit}
        tree = {m: tree[m] + moved[m ^ bit].astype(wide) for m in tree if not m & bit}
        bit = bit * 2
    d_normed = tree[0][:, :model_width]

    prob_tokens = tree[0][:, model_width : model_width + experts].T
    d_route = jnp.sum(jnp.where(named, prob_tokens[:, None, :], 0.0), axis=0)
    d_route_weight = (d_route / route_t).T.astype(short)

    gain_scaled = norm_gain[None, :] * d_normed
    centered = jnp.mean(gain_scaled * normalized, axis=1, keepdims=True)
    d_hidden = (
        layer_grad.astype(wide) + inverse * (gain_scaled - normalized * centered)
    ).astype(short)
    gain_part = jnp.sum(d_normed * normalized, axis=0)

    gain_rows = thirds(gain_part[None, :], model_width)
    blocks = {0: jnp.concatenate([d_hidden, gain_rows], axis=0)}
    for k in reversed(range(log2(head_size))):
        blocks.update({m ^ (1 << k): flipped(v, "head", 1 << k) for m, v in blocks.items()})
    gains = jnp.zeros((head_size, model_width), wide)
    for m, value in blocks.items():
        spot = head_place ^ m
        gains = lax.dynamic_update_slice(gains, joined_thirds(value[tok:], 1, model_width), (spot, 0))
    cotangent = jnp.concatenate([blocks[m][:tok] for m in range(head_size)], axis=0)
    grad = sorted_blocks(dot_nn(cotangent, out_weight, short))
    grad_wide = grad.astype(wide)
    grad_start = (grad_wide * from_start).astype(short)
    local_adjoint = dot_tn(grad_start, state_output, short)

    block = model_width // seq_size
    chosen_cot = {}
    for m in range(inner_seq):
        columns = [
            lax.dynamic_slice(
                cotangent, (0, (o * inner_seq + (inner_place ^ m)) * block), (seq_rows, block)
            )
            for o in range(outer_seq)
        ]
        chosen_cot[m] = jnp.concatenate(columns, axis=1)
    adjoints = [local_adjoint] + [flipped(local_adjoint, "seq", m) for m in range(1, inner_seq)]
    adjoint = combined(adjoints, adjoint_columns, 0, 2)
    joined = combined(adjoints, adjoint_columns, 1, 2).astype(short)
    later = [shifted(joined, "seq", -k * inner_seq) for k in range(1, outer_seq)]
    part_y = tied(y_sorted, local_adjoint)
    sent_products = [dot_tn(part_y, chosen_cot[m], short) for m in range(1, inner_seq)]
    moved = [flipped(v, "seq", m + 1) for m, v in enumerate(sent_products)]
    dx_inner, later_sum, earlier_sum, db_inner, dc_inner = scan_backward(
        state_input, state_output, scan_input, grad, cumulative_t, cumulative,
        sent_products[0], joined,
    )
    other_terms = flipped(tied(other_terms, cotangent), "head", 1)
    product = dot_tn(tied(part_y, joined), chosen_cot[0])
    for value in moved:
        product = product + value.astype(wide)
    adjoint = tied(adjoint, dx_inner) + combined(later, adjoint_columns, 2 * inner_seq, 1)
    adjoint_short = adjoint.astype(short)
    grad_wide = tied(grad, adjoint_short).astype(wide)
    product_short = product.astype(short)
    moved = []
    for m in range(1, outer_seq):
        piece = lax.dynamic_slice(
            product_short, (0, (outer_place ^ m) * block), (inner_width, block)
        )
        moved.append(flipped(piece, "seq", m * inner_seq))

    read_adjoint = dot_nt(state_input, adjoint_short) * to_end
    d_scan_input = (dx_inner + read_adjoint + skip_row * grad_wide).astype(short)
    input_part = db_inner + dot_nn(values_end, adjoint_short)
    output_part = dc_inner + dot_nn((grad_wide * from_start).astype(short), state_short)
    shared = jnp.concatenate([input_part, output_part], axis=0).astype(short)
    d_gate_weight, d_up_weight, d_down_weight = weight_terms(
        *kept, 0, (other_terms,), [shared]
    )
    for k in range(log2(head_size)):
        other = flipped(shared, "head", 1 << k)
        shared = shared + other
    shared = shared.astype(wide)
    d_out = lax.dynamic_slice(product, (0, outer_place * block), (inner_width, block))
    d_out = tied(d_out, d_down_weight)
    for value in moved:
        d_out = d_out + value.astype(wide)
    d_out_weight = d_out.T.astype(short)
    d_state_input, d_state_output = shared[:seq_rows], shared[seq_rows:]

    def head_sum(value):
        return jnp.dot(value, expand.T, precision=highest)

    skip_part = jnp.sum(head_sum(values * grad_wide), axis=0)
    skip_part = jnp.pad(skip_part, (0, lanes - heads_local))
    tail_sum = jnp.concatenate([jnp.sum(gains, axis=0), skip_part], axis=0)
    tail_sum = summed(tied(tail_sum, adjoint_short), "seq")
    d_norm_gain = tail_sum[:model_width]
    d_skip_gain = tail_sum[model_width : model_width + heads_local]
    growth = jnp.exp(total_decay)
    from_past = head_sum(read_state * grad_wide)
    to_future = head_sum(read_adjoint * values)
    corner = growth * jnp.sum(
        (state_in * adjoint).reshape(heads_local, head_dim * state_input.shape[1]), axis=1
    )
    forward_part = later_sum.T - earlier_sum + from_past
    d_log_decay = (
        lax.dot_general(
            lower_ones, forward_part, (((0,), (0,)), ((), ())),
            precision=highest, preferred_element_type=wide,
        )
        + jnp.dot(lower_ones - jnp.eye(seq_rows, dtype=wide), to_future, precision=highest)
        + corner[None, :]
    )
    return (
        d_hidden,
        d_norm_gain,
        d_route_weight,
        d_gate_weight,
        d_up_weight,
        d_down_weight,
        d_out_weight,
        d_scan_input,
        d_state_input,
        d_state_output,
        d_log_decay,
        d_skip_gain,
    )


def solution(mesh):
    in_specs = (
        P(("seq", "head"), None),
        P(),
        P(("seq", "head"), None),
        P(("seq", "head"), None),
        P(("seq", "head"), None, None),
        P(("seq", "head"), None, None),
        P(("seq", "head"), None, None),
        P(("seq", "head"), None),
        P("seq", "head"),
        P("seq", None),
        P("seq", None),
        P("seq", "head"),
        P("head"),
        P(None, "head"),
    )
    out_specs = (
        P(("seq", "head"), None),
        P(),
        P(("seq", "head"), None),
        P(("seq", "head"), None, None),
        P(("seq", "head"), None, None),
        P(("seq", "head"), None, None),
        P("seq", "head"),
        P("seq", "head"),
        P("seq", None),
        P("seq", None),
        P("seq", "head"),
        P("head"),
    )
    return jax.shard_map(shards, mesh=mesh, in_specs=in_specs, out_specs=out_specs, check_vma=False)
```

```python
import functools

import jax
import jax.numpy as jnp
from jax import lax
from jax.experimental import pallas as pl
from jax.experimental.pallas import tpu as pltpu
from jax.sharding import PartitionSpec as P

highest = lax.Precision.HIGHEST
epsilon = 1e-06
wide = jnp.float32
short = jnp.bfloat16
both = ("seq", "head")


def log2(number):
    return number.bit_length() - 1


def flipped(value, axis, mask):
    names = axis if isinstance(axis, tuple) else (axis,)
    size = 1
    for name in names:
        size = size * lax.axis_size(name)
    return lax.ppermute(value, axis, [(i, i ^ mask) for i in range(size)])


def shifted(value, axis, distance):
    size = lax.axis_size(axis)
    pairs = [(i, i + distance) for i in range(size) if 0 <= i + distance < size]
    return lax.ppermute(value, axis, pairs)


def summed(value, axis):
    size = lax.axis_size(axis)
    for bit in range(log2(size)):
        value = value + flipped(value, axis, 1 << bit)
    return value


light = pl.CostEstimate(flops=1, bytes_accessed=1, transcendentals=0)


def untouched(*refs):
    pass


def tied(value, *others):
    anywhere = pl.BlockSpec(memory_space=pl.ANY)
    return pl.pallas_call(
        untouched,
        out_shape=jax.ShapeDtypeStruct(value.shape, value.dtype),
        in_specs=[anywhere] * (1 + len(others)),
        out_specs=anywhere,
        input_output_aliases={0: 0},
        cost_estimate=light,
    )(value, *others)


def dot_nn(a, b, out=wide):
    return lax.dot_general(a, b, (((1,), (0,)), ((), ())), preferred_element_type=out)


def dot_nt(a, b, out=wide):
    return lax.dot_general(a, b, (((1,), (1,)), ((), ())), preferred_element_type=out)


def dot_tn(a, b, out=wide):
    return lax.dot_general(a, b, (((0,), (0,)), ((), ())), preferred_element_type=out)


def forward_kernel(heads, b_ref, c_ref, x_ref, row_ref, col_ref, y_ref, score_ref):
    step = pl.program_id(0)
    rows = b_ref.shape[0]

    @pl.when(step == 0)
    def _():
        score_ref[...] = dot_nt(c_ref[...], b_ref[...])

    scores = score_ref[...]
    keep = lax.broadcasted_iota(jnp.int32, (rows, rows), 0) >= lax.broadcasted_iota(
        jnp.int32, (rows, rows), 1
    )
    block = x_ref[...]
    width = block.shape[1]
    lane = lax.broadcasted_iota(jnp.int32, (rows, width), 1)
    head_lane = lax.broadcasted_iota(jnp.int32, col_ref.shape, 1)
    total = jnp.zeros((rows, width), wide)
    for k in range(heads):
        head = step * heads + k
        column = jnp.sum(jnp.where(head_lane == head, col_ref[...], 0.0), axis=1, keepdims=True)
        line = row_ref[pl.ds(head, 1), :]
        decay = jnp.where(keep, jnp.exp(jnp.minimum(column - line, 0.0)), 0.0)
        mine = (lane // (width // heads)) == k
        total = total + dot_nn(
            (decay * scores).astype(short), jnp.where(mine, block, jnp.zeros_like(block))
        )
    y_ref[...] = total


def backward_kernel(
    heads, b_ref, c_ref, x_ref, g_ref, row_ref, col_ref, *refs
):
    dx_ref, tsum_ref, ssum_ref, db_ref, dc_ref, score_ref, mask_ref = refs[-7:]
    step = pl.program_id(0)
    rows = b_ref.shape[0]

    @pl.when(step == 0)
    def _():
        score_ref[...] = dot_nt(b_ref[...], c_ref[...])
        mask_ref[...] = jnp.zeros_like(mask_ref)
        ssum_ref[...] = jnp.zeros_like(ssum_ref)

    scores = score_ref[...]
    keep = lax.broadcasted_iota(jnp.int32, (rows, rows), 0) <= lax.broadcasted_iota(
        jnp.int32, (rows, rows), 1
    )
    values = x_ref[...]
    grads = g_ref[...]
    width = values.shape[1]
    lane = lax.broadcasted_iota(jnp.int32, (rows, width), 1)
    head_lane = lax.broadcasted_iota(jnp.int32, col_ref.shape, 1)
    total = jnp.zeros((rows, width), wide)
    for k in range(heads):
        head = step * heads + k
        column = jnp.sum(jnp.where(head_lane == head, col_ref[...], 0.0), axis=1, keepdims=True)
        line = row_ref[pl.ds(head, 1), :]
        decay = jnp.where(keep, jnp.exp(jnp.minimum(line - column, 0.0)), 0.0)
        mine = (lane // (width // heads)) == k
        head_grads = jnp.where(mine, grads, jnp.zeros_like(grads))
        pair = decay * dot_nt(values, head_grads)
        mask_ref[...] += pair
        full = pair * scores
        tsum_ref[pl.ds(head, 1), :] = jnp.sum(full, axis=0, keepdims=True)
        ssum_ref[...] += jnp.where(head_lane == head, jnp.sum(full, axis=1, keepdims=True), 0.0)
        total = total + dot_nn((decay * scores).astype(short), head_grads)
    dx_ref[...] = total

    @pl.when(step == pl.num_programs(0) - 1)
    def _():
        mask = mask_ref[...].astype(short)
        db_ref[...] = dot_nn(mask, c_ref[...])
        dc_ref[...] = dot_tn(mask, b_ref[...])


inside = pl.BlockSpec(memory_space=pltpu.VMEM)
anywhere = pl.BlockSpec(memory_space=pl.ANY)
scalars = pl.BlockSpec(memory_space=pltpu.SMEM)
lanes = 128
mega = 1024 * 1024


def pack_kernel(count, cap, tok, experts, pick_ref, bundle_ref, *refs):
    outs, hit_ref = refs[-1 - count : -1], refs[-1]
    width = bundle_ref.shape[1]
    tail = bundle_ref[2 * tok :, :]
    table = [tail[:, i * tok : (i + 1) * tok] for i in range(2 * experts // 16)]
    table = jnp.concatenate(table, axis=0).astype(wide)
    line = lax.broadcasted_iota(jnp.int32, (experts, tok), 0)
    slot = lax.broadcasted_iota(jnp.int32, (cap, tok), 0).astype(wide)
    plain, scaled = [], []
    for k in range(count):
        mine = line == pick_ref[k]
        rank = jnp.sum(jnp.where(mine, table[:experts], 0.0), axis=0, keepdims=True)
        scale = jnp.sum(jnp.where(mine, table[experts:], 0.0), axis=0, keepdims=True)
        plain.append(jnp.where(rank == slot, 1.0, 0.0))
        scaled.append(jnp.where(rank == slot, scale, 0.0))
    plain = jnp.concatenate(plain, axis=0).astype(short)
    scaled = jnp.concatenate(scaled, axis=0).astype(short)
    hit_ref[...] = plain
    rows = dot_nn(plain, bundle_ref[:tok, :])
    grads = dot_nn(scaled, bundle_ref[tok : 2 * tok, :])
    for k in range(count):
        outs[k][:, :width] = rows[k * cap : (k + 1) * cap].astype(short)
        outs[k][:, width:] = grads[k * cap : (k + 1) * cap].astype(short)


def pack(pick, bundle, cap, tok, experts, ties):
    count, width = pick.shape[0], bundle.shape[1]
    out = pl.pallas_call(
        functools.partial(pack_kernel, count, cap, tok, experts),
        in_specs=[scalars, inside] + [anywhere] * len(ties),
        out_specs=[inside] * (count + 1),
        out_shape=[jax.ShapeDtypeStruct((cap, 2 * width), short)] * count
        + [jax.ShapeDtypeStruct((count * cap, tok), short)],
        compiler_params=pltpu.CompilerParams(vmem_limit_bytes=32 * mega),
        cost_estimate=light,
    )(pick, bundle, *ties)
    return list(out[:count]), out[count]


def expert_kernel(count, first, expert_ref, *refs):
    pieces, weights = refs[:count], refs[count : count + 4]
    outs = refs[-(count + 10) :]
    rows_out, outs = outs[:count], outs[count:]
    all_refs, (gu0, down0, gu1, down1), total_ref, sems = outs[:4], outs[4:8], outs[8], outs[9]
    copies = []
    for i, held in enumerate((gu0, down0, gu1, down1)):
        copies.append(pltpu.make_async_copy(weights[i], held, sems.at[i]))
        copies[i].start()
    cap = pieces[0].shape[0]
    width = pieces[0].shape[1] // 2
    half = down0.shape[0]
    both_rows = jnp.concatenate([piece[...].astype(wide) for piece in pieces], axis=0).astype(short)
    all_refs[0][...] = both_rows[:, :width]
    all_refs[1][...] = both_rows[:, width:]
    rows, grads = all_refs[0], all_refs[1]
    prob = jnp.zeros((rows.shape[0], 1), wide)
    for side in range(2):
        gate_up, down = ((gu0, down0), (gu1, down1))[side]
        copies[2 * side].wait()
        pre = dot_nn(rows[...], gate_up[...])
        copies[2 * side + 1].wait()
        back = dot_nt(grads[...], down[...])
        gate_pre, up_pre = pre[:, :half], pre[:, half:]
        sig = 1.0 / (1.0 + jnp.exp(-gate_pre))
        swish = gate_pre * sig
        active = (swish * up_pre).astype(short)
        prob = prob + jnp.sum(active.astype(wide) * back, axis=1, keepdims=True)
        held = all_refs[3]
        low = 2 * half * side
        all_refs[2][:, side * half : (side + 1) * half] = active
        d_gate = back * up_pre * sig * (1.0 + gate_pre * (1.0 - sig))
        held[:, low : low + half] = d_gate.astype(short)
        held[:, low + half : low + 2 * half] = (back * swish).astype(short)
        term = dot_nt(held[:, low : low + 2 * half], gate_up[...])
        if side == 0:
            total_ref[...] = term
        else:
            total_ref[...] += term
    lane = lax.broadcasted_iota(jnp.int32, (cap, lanes), 1)
    for k in range(count):
        span = slice(k * cap, (k + 1) * cap)
        rows_out[k][:, :width] = total_ref[span, :].astype(short)
        rows_out[k][:, width:] = jnp.where(lane == expert_ref[0], prob[span], 0.0).astype(short)


def expert_rows(expert, pieces, weights, index, blocks, kept, ties):
    count, cap = len(pieces), pieces[0].shape[0]
    width = pieces[0].shape[1] // 2
    rows = count * cap
    half = weights[0][1].shape[0]
    widths = (width, width, 2 * half, 4 * half)
    given = list(kept) if kept else []
    aliases = {1 + count + 4 + i: count + i for i in range(len(given))}
    out = pl.pallas_call(
        functools.partial(expert_kernel, count, not kept),
        grid=(1,),
        in_specs=[scalars]
        + [pl.BlockSpec((cap, 2 * width), lambda i: (0, 0))] * count
        + [anywhere] * (4 + len(given) + len(ties)),
        out_specs=[pl.BlockSpec((cap, width + lanes), lambda i: (0, 0))] * count
        + [pl.BlockSpec((rows, w), lambda i: (index, 0)) for w in widths],
        out_shape=[jax.ShapeDtypeStruct((cap, width + lanes), short)] * count
        + [jax.ShapeDtypeStruct((blocks * rows, w), short) for w in widths],
        scratch_shapes=[
            pltpu.VMEM((width, 2 * half), short),
            pltpu.VMEM((half, width), short),
            pltpu.VMEM((width, 2 * half), short),
            pltpu.VMEM((half, width), short),
            pltpu.VMEM((rows, width), wide),
            pltpu.SemaphoreType.DMA((4,)),
        ],
        input_output_aliases=aliases,
        compiler_params=pltpu.CompilerParams(vmem_limit_bytes=48 * mega),
        cost_estimate=light,
    )(expert, *pieces, *weights[0], *weights[1], *given, *ties)
    return out[:count], out[count:]


def weight_kernel(joined, rows_ref, grads_ref, act_ref, pre_ref, *refs):
    up = dot_tn(rows_ref[...], pre_ref[...])
    half = act_ref.shape[1]
    if joined:
        gate_out, up_out, down_out = refs[-3:]
        other = refs[0][...].astype(wide)
        up = up + other[:, : 2 * half]
        down = dot_tn(act_ref[...], grads_ref[...]) + other[:, 2 * half :].T
        gate_out[0] = up[:, :half].astype(short)
        up_out[0] = up[:, half:].astype(short)
        down_out[0] = down.astype(short)
    else:
        refs[-1][:, : 2 * half] = up.astype(short)
        refs[-1][:, 2 * half :] = dot_tn(grads_ref[...], act_ref[...]).astype(short)


def weight_terms(rows, grads, active, pre, side, others, ties):
    count, width = rows.shape
    half = active.shape[1] // 2
    tile = min(512, width)
    column = pl.BlockSpec((count, tile), lambda i: (0, i))
    in_specs = [column, column]
    in_specs.append(pl.BlockSpec((count, half), lambda i: (0, side)))
    in_specs.append(pl.BlockSpec((count, 2 * half), lambda i: (0, side)))
    term_spec = pl.BlockSpec((tile, 3 * half), lambda i: (i, 0))
    if others:
        in_specs.append(term_spec)
        out_specs = [pl.BlockSpec((1, tile, half), lambda i: (0, i, 0))] * 2
        out_specs.append(pl.BlockSpec((1, half, tile), lambda i: (0, 0, i)))
        out_shape = [(1, width, half), (1, width, half), (1, half, width)]
    else:
        out_specs = [term_spec]
        out_shape = [(width, 3 * half)]
    return pl.pallas_call(
        functools.partial(weight_kernel, bool(others)),
        grid=(width // tile,),
        in_specs=in_specs + [anywhere] * len(ties),
        out_specs=out_specs,
        out_shape=[jax.ShapeDtypeStruct(v, short) for v in out_shape],
        compiler_params=pltpu.CompilerParams(vmem_limit_bytes=40 * mega),
        cost_estimate=light,
    )(rows, grads, active, pre, *others, *ties)


def scan_blocks(rows, state, width, heads_local):
    whole = pl.BlockSpec((rows, state), lambda i: (0, 0))
    column = pl.BlockSpec((rows, width), lambda i: (0, i))
    lines = pl.BlockSpec((heads_local, rows), lambda i: (0, 0))
    columns = pl.BlockSpec((rows, heads_local), lambda i: (0, 0))
    return whole, column, lines, columns


def scan_forward(b, c, x, lines, columns):
    rows, state = b.shape
    inner = x.shape[1]
    heads_local = columns.shape[1]
    width = 2 * (inner // heads_local)
    whole, column, line_spec, column_spec = scan_blocks(rows, state, width, heads_local)
    return pl.pallas_call(
        functools.partial(forward_kernel, 2),
        grid=(heads_local // 2,),
        in_specs=[whole, whole, column, line_spec, column_spec],
        out_specs=column,
        out_shape=jax.ShapeDtypeStruct((rows, inner), wide),
        scratch_shapes=[pltpu.VMEM((rows, rows), wide)],
        compiler_params=pltpu.CompilerParams(vmem_limit_bytes=24 * 1024 * 1024),
        cost_estimate=light,
    )(b, c, x, lines, columns)


def scan_backward(b, c, x, g, lines, columns, *ties):
    rows, state = b.shape
    inner = x.shape[1]
    heads_local = columns.shape[1]
    width = 2 * (inner // heads_local)
    whole, column, line_spec, column_spec = scan_blocks(rows, state, width, heads_local)
    return pl.pallas_call(
        functools.partial(backward_kernel, 2),
        grid=(heads_local // 2,),
        in_specs=[whole, whole, column, column, line_spec, column_spec]
        + [pl.BlockSpec(memory_space=pl.ANY)] * len(ties),
        out_specs=[column, line_spec, column_spec, whole, whole],
        out_shape=[
            jax.ShapeDtypeStruct((rows, inner), wide),
            jax.ShapeDtypeStruct((heads_local, rows), wide),
            jax.ShapeDtypeStruct((rows, heads_local), wide),
            jax.ShapeDtypeStruct((rows, state), wide),
            jax.ShapeDtypeStruct((rows, state), wide),
        ],
        scratch_shapes=[pltpu.VMEM((rows, rows), wide), pltpu.VMEM((rows, rows), wide)],
        compiler_params=pltpu.CompilerParams(vmem_limit_bytes=32 * 1024 * 1024),
        cost_estimate=pl.CostEstimate(flops=2 * 10**9, bytes_accessed=1, transcendentals=0),
    )(b, c, x, g, lines, columns, *ties)


def shards(
    hidden,
    norm_gain,
    expert_choice,
    route_weight,
    gate_weight,
    up_weight,
    down_weight,
    layer_grad,
    scan_input,
    state_input,
    state_output,
    log_decay,
    skip_gain,
    out_weight,
):
    seq_size, head_size = lax.axis_size("seq"), lax.axis_size("head")
    devices = seq_size * head_size
    experts = devices // 2
    tok, model_width = hidden.shape
    top_count = expert_choice.shape[1]
    cap = 9 * tok * top_count // (8 * experts)
    cap = (cap + 7) // 8 * 8
    groups = 1 << ((log2(devices)) // 2)
    plane = devices // groups
    plane_experts = plane // 2
    seq_place, head_place = lax.axis_index("seq"), lax.axis_index("head")
    place = seq_place * head_size + head_place
    group = place // plane

    def across(value, mask):
        return flipped(value, both, mask * plane)

    def spread(first):
        rows = [first]
        for m in range(1, groups):
            low = m & -m
            rows.append(across(rows[m ^ low], low))
        return rows

    chip = (place % plane) // 2

    def within(value, mask):
        return flipped(value, both, 2 * mask)

    seq_rows, inner_width = scan_input.shape
    heads_local = log_decay.shape[1]
    head_dim = inner_width // heads_local
    inner_seq = 1 << (log2(seq_size) // 2)
    outer_seq = seq_size // inner_seq
    inner_place, outer_place = seq_place % inner_seq, seq_place // inner_seq

    choice_t = expert_choice.T
    named = choice_t[None, :, :] == jnp.arange(experts, dtype=jnp.int32)[:, None, None]
    chosen = jnp.any(named, axis=1)
    before = jnp.arange(tok)[:, None] < jnp.arange(tok)[None, :]
    rank = dot_nn(chosen.astype(short), before.astype(short))
    rank = jnp.where(chosen, rank, -1.0).astype(short)
    route_t = route_weight.T.astype(wide)
    prob = jnp.sum(jnp.where(named, route_t[None], 0.0), axis=1).astype(short)
    tables = jnp.concatenate([rank, prob], axis=0)
    pieces = [tables[i : i + 16] for i in range(0, 2 * experts, 16)]
    pieces.append(jnp.zeros((16, model_width - tok * len(pieces)), short))
    table_rows = jnp.concatenate(pieces, axis=1)

    hidden_wide = hidden.astype(wide)
    inverse = lax.rsqrt(jnp.mean(hidden_wide * hidden_wide, axis=1, keepdims=True) + epsilon)
    normalized = hidden_wide * inverse
    normed = (normalized * norm_gain[None, :]).astype(short)
    bundles = spread(jnp.concatenate([normed, layer_grad, table_rows], axis=0))

    gate_up = jnp.concatenate([gate_weight[0], up_weight[0]], axis=1)

    order = jnp.arange(plane_experts, dtype=jnp.int32) ^ chip
    selected = group * plane_experts + order
    own_expert = selected[:1]

    hits, received, returning = [], [], []
    kept = None

    packed = []

    def prepare(m):
        ties = []
        if m == 1:
            ties = [received[0][1]]
        elif m == 2:
            ties = [received[1][1]]
        elif m > 2:
            ties = [*received[m - 2], returning[m - 3][0]]
        sent, hit = pack(selected, bundles[m], cap, tok, experts, ties)
        hits.append(hit)
        packed.append(sent)

    def send(m):
        pieces = [packed[m][0]]
        for k in range(1, plane_experts):
            outgoing = packed[m][k]
            if m == groups - 1 and k == plane_experts - 1:
                outgoing = tied(outgoing, returning[m - 2][0])
            pieces.append(within(outgoing, k))
        received.append(pieces)

    def work(m, kept):
        ties = [hits[m + 2]] if 1 <= m < groups - 2 else []
        rows, kept = expert_rows(own_expert, received[m], weights, m, groups, kept, ties)
        returning.append(rows)
        return kept

    for m in range(min(3, groups)):
        prepare(m)
        send(m)
    weights = [(gate_up, down_weight[0])]
    weights.append(
        (
            flipped(tied(gate_up, *received[0][1:]), "head", 1),
            flipped(tied(down_weight[0], *received[0][1:]), "head", 1),
        )
    )

    lower = jnp.arange(seq_rows)[:, None] >= jnp.arange(seq_rows)[None, :]
    lower_ones = lower.astype(wide)
    cumulative = jnp.dot(lower_ones, log_decay, precision=highest)
    cumulative_t = cumulative.T
    total_decay = cumulative[-1]
    head_of = (jnp.arange(inner_width) // head_dim)[None, :] == jnp.arange(heads_local)[:, None]
    expand = head_of.astype(wide)

    def expanded(value):
        return jnp.dot(value, expand, precision=highest)

    from_start = expanded(jnp.exp(cumulative))
    to_end = expanded(jnp.exp(total_decay[None, :] - cumulative))
    skip_row = expanded(skip_gain[None, :])
    values = scan_input.astype(wide)
    values_end = (values * to_end).astype(short)
    def columns_of(logs, valid):
        factors = jnp.exp(jnp.minimum(jnp.stack(logs, axis=0), 0.0))
        factors = jnp.where(jnp.stack([jnp.asarray(v) for v in valid])[:, None], factors, 0.0)
        return lax.dot_general(
            expand, factors, (((0,), (1,)), ((), ())), precision=highest,
            preferred_element_type=wide,
        )

    def combined(pieces, columns, first, step):
        total = jnp.zeros((inner_width, state_input.shape[1]), wide)
        for k, piece in enumerate(pieces):
            place_of = first + step * k
            total = total + columns[:, place_of : place_of + 1] * piece.astype(wide)
        return total

    def thirds(value, width):
        high = lax.reduce_precision(value, 8, 7)
        middle = lax.reduce_precision(value - high, 8, 7)
        rows = jnp.concatenate([high, middle, value - high - middle], axis=0)
        below = (rows.shape[0] + 15) // 16 * 16 - rows.shape[0]
        return jnp.pad(rows, ((0, below), (0, width - rows.shape[1]))).astype(short)

    def joined_thirds(rows, count, width):
        rows = rows[: 3 * count, :width].astype(wide)
        return rows[:count] + rows[count : 2 * count] + rows[2 * count :]

    start = outer_place * inner_seq
    local_state = tied(dot_tn(values_end, state_input, short), received[0][1])
    message = jnp.concatenate([local_state, thirds(total_decay[None, :], lanes)], axis=0)
    messages = [message] + [flipped(message, "seq", m) for m in range(1, inner_seq)]
    inner_totals = jnp.zeros((inner_seq, heads_local), wide)
    for m in range(inner_seq):
        piece = joined_thirds(messages[m][inner_width:], 1, heads_local)
        inner_totals = lax.dynamic_update_slice(inner_totals, piece, (inner_place ^ m, 0))
    inner_ended = jnp.concatenate(
        [jnp.zeros((1, heads_local), wide), jnp.cumsum(inner_totals, axis=0)], axis=0
    )

    def inner_before(index):
        return lax.dynamic_index_in_dim(inner_ended, index, 0, False)

    logs, valid = [], []
    for m in range(inner_seq):
        source = inner_place ^ m
        logs.append(inner_before(inner_place) - inner_before(source + 1))
        logs.append(inner_before(inner_seq) - inner_before(source + 1))
        valid.extend([source < inner_place, True])
    columns = columns_of(logs, valid)
    states = [v[:inner_width] for v in messages]
    state_in = combined(states, columns, 0, 2)
    for m in range(min(2, groups)):
        if 3 <= m + 2 < groups:
            prepare(m + 2)
        kept = work(m, kept)
        if 3 <= m + 2 < groups:
            send(m + 2)

    message = jnp.concatenate(
        [combined(states, columns, 1, 2).astype(short), thirds(inner_totals, lanes)], axis=0
    )
    message = tied(message, received[-1][1])
    messages = [message] + [flipped(message, "seq", m * inner_seq) for m in range(1, outer_seq)]
    totals = jnp.zeros((seq_size, heads_local), wide)
    for m in range(outer_seq):
        piece = joined_thirds(messages[m][inner_width:], inner_seq, heads_local)
        totals = lax.dynamic_update_slice(totals, piece, ((outer_place ^ m) * inner_seq, 0))
    ended = jnp.concatenate(
        [jnp.zeros((1, heads_local), wide), jnp.cumsum(totals, axis=0)], axis=0
    )

    def before_of(index):
        return lax.dynamic_index_in_dim(ended, jnp.clip(index, 0, seq_size), 0, False)

    logs, valid = [], []
    for m in range(1, outer_seq):
        source = outer_place ^ m
        logs.append(before_of(seq_place) - before_of((source + 1) * inner_seq))
        valid.append(source < outer_place)
    columns = columns_of(logs, valid)
    state_in = state_in + combined([v[:inner_width] for v in messages[1:]], columns, 0, 1)

    logs, valid = [], []
    for m in range(inner_seq):
        source = start + (inner_place ^ m)
        logs.append(before_of(source) - before_of(seq_place + 1))
        logs.append(before_of(source) - before_of(start))
        valid.extend([source > seq_place, True])
    for k in range(1, outer_seq):
        logs.append(before_of(start + k * inner_seq) - before_of(seq_place + 1))
        valid.append(True)
    adjoint_columns = columns_of(logs, valid)

    state_short = state_in.astype(short)
    read_state = dot_nt(state_output, state_short) * from_start
    y_inner = scan_forward(state_input, state_output, scan_input, cumulative_t, cumulative)
    y_rounded = (y_inner + read_state + skip_row * values).astype(short)


    for m in range(2, groups):
        if m + 2 < groups:
            prepare(m + 2)
        kept = work(m, kept)
        if m + 2 < groups:
            send(m + 2)

    partial = [None] * groups
    for m in reversed(range(groups)):
        outgoing = list(returning[m])
        if m < groups - 1:
            after = partial[m + 2] if m < groups - 2 else returning[groups - 1][0]
            outgoing = outgoing[:1] + [tied(v, after) for v in outgoing[1:]]
        back = outgoing[:1] + [within(outgoing[k], k) for k in range(1, plane_experts)]
        partial[m] = dot_tn(hits[m], jnp.concatenate(back, axis=0))

    def sorted_blocks(value):
        width = value.shape[1]
        return jnp.concatenate(
            [
                lax.dynamic_slice(value, ((head_place ^ n) * tok, 0), (tok, width))
                for n in range(head_size)
            ],
            axis=0,
        )

    y_sorted = sorted_blocks(y_rounded)

    other_terms = weight_terms(*kept, 1, (), [partial[0], y_sorted])[0]
    partial[0] = tied(partial[0], other_terms)

    bit = 1
    tree = {m: partial[m] for m in range(groups)}
    while bit < groups:
        moved = {m: across(tree[m].astype(short), bit) for m in tree if m & bit}
        tree = {m: tree[m] + moved[m ^ bit].astype(wide) for m in tree if not m & bit}
        bit = bit * 2
    d_normed = tree[0][:, :model_width]

    prob_tokens = tree[0][:, model_width : model_width + experts].T
    d_route = jnp.sum(jnp.where(named, prob_tokens[:, None, :], 0.0), axis=0)
    d_route_weight = (d_route / route_t).T.astype(short)

    gain_scaled = norm_gain[None, :] * d_normed
    centered = jnp.mean(gain_scaled * normalized, axis=1, keepdims=True)
    d_hidden = (
        layer_grad.astype(wide) + inverse * (gain_scaled - normalized * centered)
    ).astype(short)
    gain_part = jnp.sum(d_normed * normalized, axis=0)

    gain_rows = thirds(gain_part[None, :], model_width)
    blocks = {0: jnp.concatenate([d_hidden, gain_rows], axis=0)}
    for k in reversed(range(log2(head_size))):
        blocks.update({m ^ (1 << k): flipped(v, "head", 1 << k) for m, v in blocks.items()})
    gains = jnp.zeros((head_size, model_width), wide)
    for m, value in blocks.items():
        spot = head_place ^ m
        gains = lax.dynamic_update_slice(gains, joined_thirds(value[tok:], 1, model_width), (spot, 0))
    cotangent = jnp.concatenate([blocks[m][:tok] for m in range(head_size)], axis=0)
    near = head_size // 2
    grad = [
        dot_nn(jnp.concatenate([blocks[m][:tok] for m in part], axis=0), out_weight, short)
        for part in (range(near), range(near, head_size))
    ]
    grad = sorted_blocks(jnp.concatenate(grad, axis=0))
    grad_wide = grad.astype(wide)
    grad_start = (grad_wide * from_start).astype(short)
    local_adjoint = dot_tn(grad_start, state_output, short)

    block = model_width // seq_size
    chosen_cot = {}
    for m in range(inner_seq):
        columns = [
            lax.dynamic_slice(
                cotangent, (0, (o * inner_seq + (inner_place ^ m)) * block), (seq_rows, block)
            )
            for o in range(outer_seq)
        ]
        chosen_cot[m] = jnp.concatenate(columns, axis=1)
    adjoints = [local_adjoint] + [flipped(local_adjoint, "seq", m) for m in range(1, inner_seq)]
    adjoint = combined(adjoints, adjoint_columns, 0, 2)
    joined = combined(adjoints, adjoint_columns, 1, 2).astype(short)
    later = [shifted(joined, "seq", -k * inner_seq) for k in range(1, outer_seq)]
    part_y = tied(y_sorted, local_adjoint)
    sent_products = [dot_tn(part_y, chosen_cot[m], short) for m in range(1, inner_seq)]
    moved = [flipped(v, "seq", m + 1) for m, v in enumerate(sent_products)]
    dx_inner, later_sum, earlier_sum, db_inner, dc_inner = scan_backward(
        state_input, state_output, scan_input, grad, cumulative_t, cumulative,
        sent_products[0], joined,
    )
    other_terms = flipped(tied(other_terms, cotangent), "head", 1)
    product = dot_tn(tied(part_y, joined), chosen_cot[0])
    for value in moved:
        product = product + value.astype(wide)
    adjoint = tied(adjoint, dx_inner) + combined(later, adjoint_columns, 2 * inner_seq, 1)
    adjoint_short = adjoint.astype(short)
    grad_wide = tied(grad, adjoint_short).astype(wide)
    product_short = product.astype(short)
    moved = []
    for m in range(1, outer_seq):
        piece = lax.dynamic_slice(
            product_short, (0, (outer_place ^ m) * block), (inner_width, block)
        )
        moved.append(flipped(piece, "seq", m * inner_seq))

    read_adjoint = dot_nt(state_input, adjoint_short) * to_end
    d_scan_input = (dx_inner + read_adjoint + skip_row * grad_wide).astype(short)
    input_part = db_inner + dot_nn(values_end, adjoint_short)
    output_part = dc_inner + dot_nn((grad_wide * from_start).astype(short), state_short)
    shared = jnp.concatenate([input_part, output_part], axis=0).astype(short)
    d_gate_weight, d_up_weight, d_down_weight = weight_terms(
        *kept, 0, (other_terms,), [shared]
    )
    for k in range(log2(head_size)):
        other = flipped(shared, "head", 1 << k)
        shared = shared + other
    shared = shared.astype(wide)
    d_out = lax.dynamic_slice(product, (0, outer_place * block), (inner_width, block))
    d_out = tied(d_out, d_down_weight)
    for value in moved:
        d_out = d_out + value.astype(wide)
    d_out_weight = d_out.T.astype(short)
    d_state_input, d_state_output = shared[:seq_rows], shared[seq_rows:]

    def head_sum(value):
        return jnp.dot(value, expand.T, precision=highest)

    skip_part = jnp.sum(head_sum(values * grad_wide), axis=0)
    skip_part = jnp.pad(skip_part, (0, lanes - heads_local))
    tail_sum = jnp.concatenate([jnp.sum(gains, axis=0), skip_part], axis=0)
    tail_sum = summed(tied(tail_sum, adjoint_short), "seq")
    d_norm_gain = tail_sum[:model_width]
    d_skip_gain = tail_sum[model_width : model_width + heads_local]
    growth = jnp.exp(total_decay)
    from_past = head_sum(read_state * grad_wide)
    to_future = head_sum(read_adjoint * values)
    corner = growth * jnp.sum(
        (state_in * adjoint).reshape(heads_local, head_dim * state_input.shape[1]), axis=1
    )
    forward_part = later_sum.T - earlier_sum + from_past
    d_log_decay = (
        lax.dot_general(
            lower_ones, forward_part, (((0,), (0,)), ((), ())),
            precision=highest, preferred_element_type=wide,
        )
        + jnp.dot(lower_ones - jnp.eye(seq_rows, dtype=wide), to_future, precision=highest)
        + corner[None, :]
    )
    return (
        d_hidden,
        d_norm_gain,
        d_route_weight,
        d_gate_weight,
        d_up_weight,
        d_down_weight,
        d_out_weight,
        d_scan_input,
        d_state_input,
        d_state_output,
        d_log_decay,
        d_skip_gain,
    )


def solution(mesh):
    in_specs = (
        P(("seq", "head"), None),
        P(),
        P(("seq", "head"), None),
        P(("seq", "head"), None),
        P(("seq", "head"), None, None),
        P(("seq", "head"), None, None),
        P(("seq", "head"), None, None),
        P(("seq", "head"), None),
        P("seq", "head"),
        P("seq", None),
        P("seq", None),
        P("seq", "head"),
        P("head"),
        P(None, "head"),
    )
    out_specs = (
        P(("seq", "head"), None),
        P(),
        P(("seq", "head"), None),
        P(("seq", "head"), None, None),
        P(("seq", "head"), None, None),
        P(("seq", "head"), None, None),
        P("seq", "head"),
        P("seq", "head"),
        P("seq", None),
        P("seq", None),
        P("seq", "head"),
        P("head"),
    )
    return jax.shard_map(shards, mesh=mesh, in_specs=in_specs, out_specs=out_specs, check_vma=False)
```

```python
import functools

import jax
import jax.numpy as jnp
from jax import lax
from jax.experimental import pallas as pl
from jax.experimental.pallas import tpu as pltpu
from jax.sharding import PartitionSpec as P

highest = lax.Precision.HIGHEST
epsilon = 1e-06
wide = jnp.float32
short = jnp.bfloat16
both = ("seq", "head")


def log2(number):
    return number.bit_length() - 1


def flipped(value, axis, mask):
    names = axis if isinstance(axis, tuple) else (axis,)
    size = 1
    for name in names:
        size = size * lax.axis_size(name)
    return lax.ppermute(value, axis, [(i, i ^ mask) for i in range(size)])


def shifted(value, axis, distance):
    size = lax.axis_size(axis)
    pairs = [(i, i + distance) for i in range(size) if 0 <= i + distance < size]
    return lax.ppermute(value, axis, pairs)


def summed(value, axis):
    size = lax.axis_size(axis)
    for bit in range(log2(size)):
        value = value + flipped(value, axis, 1 << bit)
    return value


light = pl.CostEstimate(flops=1, bytes_accessed=1, transcendentals=0)


def untouched(*refs):
    pass


def tied(value, *others):
    anywhere = pl.BlockSpec(memory_space=pl.ANY)
    return pl.pallas_call(
        untouched,
        out_shape=jax.ShapeDtypeStruct(value.shape, value.dtype),
        in_specs=[anywhere] * (1 + len(others)),
        out_specs=anywhere,
        input_output_aliases={0: 0},
        cost_estimate=light,
    )(value, *others)


def dot_nn(a, b, out=wide):
    return lax.dot_general(a, b, (((1,), (0,)), ((), ())), preferred_element_type=out)


def dot_nt(a, b, out=wide):
    return lax.dot_general(a, b, (((1,), (1,)), ((), ())), preferred_element_type=out)


def dot_tn(a, b, out=wide):
    return lax.dot_general(a, b, (((0,), (0,)), ((), ())), preferred_element_type=out)


def forward_kernel(heads, b_ref, c_ref, x_ref, row_ref, col_ref, y_ref, score_ref):
    step = pl.program_id(0)
    rows = b_ref.shape[0]

    @pl.when(step == 0)
    def _():
        score_ref[...] = dot_nt(c_ref[...], b_ref[...])

    scores = score_ref[...]
    keep = lax.broadcasted_iota(jnp.int32, (rows, rows), 0) >= lax.broadcasted_iota(
        jnp.int32, (rows, rows), 1
    )
    block = x_ref[...]
    width = block.shape[1]
    lane = lax.broadcasted_iota(jnp.int32, (rows, width), 1)
    head_lane = lax.broadcasted_iota(jnp.int32, col_ref.shape, 1)
    total = jnp.zeros((rows, width), wide)
    for k in range(heads):
        head = step * heads + k
        column = jnp.sum(jnp.where(head_lane == head, col_ref[...], 0.0), axis=1, keepdims=True)
        line = row_ref[pl.ds(head, 1), :]
        decay = jnp.where(keep, jnp.exp(jnp.minimum(column - line, 0.0)), 0.0)
        mine = (lane // (width // heads)) == k
        total = total + dot_nn(
            (decay * scores).astype(short), jnp.where(mine, block, jnp.zeros_like(block))
        )
    y_ref[...] = total


def backward_kernel(
    heads, b_ref, c_ref, x_ref, g_ref, row_ref, col_ref, *refs
):
    dx_ref, tsum_ref, ssum_ref, db_ref, dc_ref, score_ref, mask_ref = refs[-7:]
    step = pl.program_id(0)
    rows = b_ref.shape[0]

    @pl.when(step == 0)
    def _():
        score_ref[...] = dot_nt(b_ref[...], c_ref[...])
        mask_ref[...] = jnp.zeros_like(mask_ref)
        ssum_ref[...] = jnp.zeros_like(ssum_ref)

    scores = score_ref[...]
    keep = lax.broadcasted_iota(jnp.int32, (rows, rows), 0) <= lax.broadcasted_iota(
        jnp.int32, (rows, rows), 1
    )
    values = x_ref[...]
    grads = g_ref[...]
    width = values.shape[1]
    lane = lax.broadcasted_iota(jnp.int32, (rows, width), 1)
    head_lane = lax.broadcasted_iota(jnp.int32, col_ref.shape, 1)
    total = jnp.zeros((rows, width), wide)
    for k in range(heads):
        head = step * heads + k
        column = jnp.sum(jnp.where(head_lane == head, col_ref[...], 0.0), axis=1, keepdims=True)
        line = row_ref[pl.ds(head, 1), :]
        decay = jnp.where(keep, jnp.exp(jnp.minimum(line - column, 0.0)), 0.0)
        mine = (lane // (width // heads)) == k
        head_grads = jnp.where(mine, grads, jnp.zeros_like(grads))
        pair = decay * dot_nt(values, head_grads)
        mask_ref[...] += pair
        full = pair * scores
        tsum_ref[pl.ds(head, 1), :] = jnp.sum(full, axis=0, keepdims=True)
        ssum_ref[...] += jnp.where(head_lane == head, jnp.sum(full, axis=1, keepdims=True), 0.0)
        total = total + dot_nn((decay * scores).astype(short), head_grads)
    dx_ref[...] = total

    @pl.when(step == pl.num_programs(0) - 1)
    def _():
        mask = mask_ref[...].astype(short)
        db_ref[...] = dot_nn(mask, c_ref[...])
        dc_ref[...] = dot_tn(mask, b_ref[...])


inside = pl.BlockSpec(memory_space=pltpu.VMEM)
anywhere = pl.BlockSpec(memory_space=pl.ANY)
scalars = pl.BlockSpec(memory_space=pltpu.SMEM)
lanes = 128
mega = 1024 * 1024


def pack_kernel(count, cap, tok, experts, pick_ref, bundle_ref, *refs):
    outs, hit_ref = refs[-1 - count : -1], refs[-1]
    width = bundle_ref.shape[1]
    tail = bundle_ref[2 * tok :, :]
    table = [tail[:, i * tok : (i + 1) * tok] for i in range(2 * experts // 16)]
    table = jnp.concatenate(table, axis=0).astype(wide)
    line = lax.broadcasted_iota(jnp.int32, (experts, tok), 0)
    slot = lax.broadcasted_iota(jnp.int32, (cap, tok), 0).astype(wide)
    plain, scaled = [], []
    for k in range(count):
        mine = line == pick_ref[k]
        rank = jnp.sum(jnp.where(mine, table[:experts], 0.0), axis=0, keepdims=True)
        scale = jnp.sum(jnp.where(mine, table[experts:], 0.0), axis=0, keepdims=True)
        plain.append(jnp.where(rank == slot, 1.0, 0.0))
        scaled.append(jnp.where(rank == slot, scale, 0.0))
    plain = jnp.concatenate(plain, axis=0).astype(short)
    scaled = jnp.concatenate(scaled, axis=0).astype(short)
    hit_ref[...] = plain
    rows = dot_nn(plain, bundle_ref[:tok, :])
    grads = dot_nn(scaled, bundle_ref[tok : 2 * tok, :])
    for k in range(count):
        outs[k][:, :width] = rows[k * cap : (k + 1) * cap].astype(short)
        outs[k][:, width:] = grads[k * cap : (k + 1) * cap].astype(short)


def pack(pick, bundle, cap, tok, experts, ties):
    count, width = pick.shape[0], bundle.shape[1]
    out = pl.pallas_call(
        functools.partial(pack_kernel, count, cap, tok, experts),
        in_specs=[scalars, inside] + [anywhere] * len(ties),
        out_specs=[inside] * (count + 1),
        out_shape=[jax.ShapeDtypeStruct((cap, 2 * width), short)] * count
        + [jax.ShapeDtypeStruct((count * cap, tok), short)],
        compiler_params=pltpu.CompilerParams(vmem_limit_bytes=32 * mega),
        cost_estimate=light,
    )(pick, bundle, *ties)
    return list(out[:count]), out[count]


def expert_kernel(count, first, expert_ref, *refs):
    pieces, weights = refs[:count], refs[count : count + 4]
    outs = refs[-(count + 10) :]
    rows_out, outs = outs[:count], outs[count:]
    all_refs, (gu0, down0, gu1, down1), total_ref, sems = outs[:4], outs[4:8], outs[8], outs[9]
    copies = []
    for i, held in enumerate((gu0, down0, gu1, down1)):
        copies.append(pltpu.make_async_copy(weights[i], held, sems.at[i]))
        copies[i].start()
    cap = pieces[0].shape[0]
    width = pieces[0].shape[1] // 2
    half = down0.shape[0]
    both_rows = jnp.concatenate([piece[...].astype(wide) for piece in pieces], axis=0).astype(short)
    all_refs[0][...] = both_rows[:, :width]
    all_refs[1][...] = both_rows[:, width:]
    rows, grads = all_refs[0], all_refs[1]
    prob = jnp.zeros((rows.shape[0], 1), wide)
    for side in range(2):
        gate_up, down = ((gu0, down0), (gu1, down1))[side]
        copies[2 * side].wait()
        pre = dot_nn(rows[...], gate_up[...])
        copies[2 * side + 1].wait()
        back = dot_nt(grads[...], down[...])
        gate_pre, up_pre = pre[:, :half], pre[:, half:]
        sig = 1.0 / (1.0 + jnp.exp(-gate_pre))
        swish = gate_pre * sig
        active = (swish * up_pre).astype(short)
        prob = prob + jnp.sum(active.astype(wide) * back, axis=1, keepdims=True)
        held = all_refs[3]
        low = 2 * half * side
        all_refs[2][:, side * half : (side + 1) * half] = active
        d_gate = back * up_pre * sig * (1.0 + gate_pre * (1.0 - sig))
        held[:, low : low + half] = d_gate.astype(short)
        held[:, low + half : low + 2 * half] = (back * swish).astype(short)
        term = dot_nt(held[:, low : low + 2 * half], gate_up[...])
        if side == 0:
            total_ref[...] = term
        else:
            total_ref[...] += term
    lane = lax.broadcasted_iota(jnp.int32, (cap, lanes), 1)
    for k in range(count):
        span = slice(k * cap, (k + 1) * cap)
        rows_out[k][:, :width] = total_ref[span, :].astype(short)
        rows_out[k][:, width:] = jnp.where(lane == expert_ref[0], prob[span], 0.0).astype(short)


def expert_rows(expert, pieces, weights, index, blocks, kept, ties):
    count, cap = len(pieces), pieces[0].shape[0]
    width = pieces[0].shape[1] // 2
    rows = count * cap
    half = weights[0][1].shape[0]
    widths = (width, width, 2 * half, 4 * half)
    given = list(kept) if kept else []
    aliases = {1 + count + 4 + i: count + i for i in range(len(given))}
    out = pl.pallas_call(
        functools.partial(expert_kernel, count, not kept),
        grid=(1,),
        in_specs=[scalars]
        + [pl.BlockSpec((cap, 2 * width), lambda i: (0, 0))] * count
        + [anywhere] * (4 + len(given) + len(ties)),
        out_specs=[pl.BlockSpec((cap, width + lanes), lambda i: (0, 0))] * count
        + [pl.BlockSpec((rows, w), lambda i: (index, 0)) for w in widths],
        out_shape=[jax.ShapeDtypeStruct((cap, width + lanes), short)] * count
        + [jax.ShapeDtypeStruct((blocks * rows, w), short) for w in widths],
        scratch_shapes=[
            pltpu.VMEM((width, 2 * half), short),
            pltpu.VMEM((half, width), short),
            pltpu.VMEM((width, 2 * half), short),
            pltpu.VMEM((half, width), short),
            pltpu.VMEM((rows, width), wide),
            pltpu.SemaphoreType.DMA((4,)),
        ],
        input_output_aliases=aliases,
        compiler_params=pltpu.CompilerParams(vmem_limit_bytes=48 * mega),
        cost_estimate=light,
    )(expert, *pieces, *weights[0], *weights[1], *given, *ties)
    return out[:count], out[count:]


def weight_kernel(joined, rows_ref, grads_ref, act_ref, pre_ref, *refs):
    up = dot_tn(rows_ref[...], pre_ref[...])
    half = act_ref.shape[1]
    if joined:
        gate_out, up_out, down_out = refs[-3:]
        other = refs[0][...].astype(wide)
        up = up + other[:, : 2 * half]
        down = dot_tn(act_ref[...], grads_ref[...]) + other[:, 2 * half :].T
        gate_out[0] = up[:, :half].astype(short)
        up_out[0] = up[:, half:].astype(short)
        down_out[0] = down.astype(short)
    else:
        refs[-1][:, : 2 * half] = up.astype(short)
        refs[-1][:, 2 * half :] = dot_tn(grads_ref[...], act_ref[...]).astype(short)


def weight_terms(rows, grads, active, pre, side, others, ties):
    count, width = rows.shape
    half = active.shape[1] // 2
    tile = min(512, width)
    column = pl.BlockSpec((count, tile), lambda i: (0, i))
    in_specs = [column, column]
    in_specs.append(pl.BlockSpec((count, half), lambda i: (0, side)))
    in_specs.append(pl.BlockSpec((count, 2 * half), lambda i: (0, side)))
    term_spec = pl.BlockSpec((tile, 3 * half), lambda i: (i, 0))
    if others:
        in_specs.append(term_spec)
        out_specs = [pl.BlockSpec((1, tile, half), lambda i: (0, i, 0))] * 2
        out_specs.append(pl.BlockSpec((1, half, tile), lambda i: (0, 0, i)))
        out_shape = [(1, width, half), (1, width, half), (1, half, width)]
    else:
        out_specs = [term_spec]
        out_shape = [(width, 3 * half)]
    return pl.pallas_call(
        functools.partial(weight_kernel, bool(others)),
        grid=(width // tile,),
        in_specs=in_specs + [anywhere] * len(ties),
        out_specs=out_specs,
        out_shape=[jax.ShapeDtypeStruct(v, short) for v in out_shape],
        compiler_params=pltpu.CompilerParams(vmem_limit_bytes=40 * mega),
        cost_estimate=light,
    )(rows, grads, active, pre, *others, *ties)


def scan_blocks(rows, state, width, heads_local):
    whole = pl.BlockSpec((rows, state), lambda i: (0, 0))
    column = pl.BlockSpec((rows, width), lambda i: (0, i))
    lines = pl.BlockSpec((heads_local, rows), lambda i: (0, 0))
    columns = pl.BlockSpec((rows, heads_local), lambda i: (0, 0))
    return whole, column, lines, columns


def scan_forward(b, c, x, lines, columns):
    rows, state = b.shape
    inner = x.shape[1]
    heads_local = columns.shape[1]
    width = 2 * (inner // heads_local)
    whole, column, line_spec, column_spec = scan_blocks(rows, state, width, heads_local)
    return pl.pallas_call(
        functools.partial(forward_kernel, 2),
        grid=(heads_local // 2,),
        in_specs=[whole, whole, column, line_spec, column_spec],
        out_specs=column,
        out_shape=jax.ShapeDtypeStruct((rows, inner), wide),
        scratch_shapes=[pltpu.VMEM((rows, rows), wide)],
        compiler_params=pltpu.CompilerParams(vmem_limit_bytes=24 * 1024 * 1024),
        cost_estimate=light,
    )(b, c, x, lines, columns)


def scan_backward(b, c, x, g, lines, columns, *ties):
    rows, state = b.shape
    inner = x.shape[1]
    heads_local = columns.shape[1]
    width = 2 * (inner // heads_local)
    whole, column, line_spec, column_spec = scan_blocks(rows, state, width, heads_local)
    return pl.pallas_call(
        functools.partial(backward_kernel, 2),
        grid=(heads_local // 2,),
        in_specs=[whole, whole, column, column, line_spec, column_spec]
        + [pl.BlockSpec(memory_space=pl.ANY)] * len(ties),
        out_specs=[column, line_spec, column_spec, whole, whole],
        out_shape=[
            jax.ShapeDtypeStruct((rows, inner), wide),
            jax.ShapeDtypeStruct((heads_local, rows), wide),
            jax.ShapeDtypeStruct((rows, heads_local), wide),
            jax.ShapeDtypeStruct((rows, state), wide),
            jax.ShapeDtypeStruct((rows, state), wide),
        ],
        scratch_shapes=[pltpu.VMEM((rows, rows), wide), pltpu.VMEM((rows, rows), wide)],
        compiler_params=pltpu.CompilerParams(vmem_limit_bytes=32 * 1024 * 1024),
        cost_estimate=pl.CostEstimate(flops=2 * 10**9, bytes_accessed=1, transcendentals=0),
    )(b, c, x, g, lines, columns, *ties)


def shards(
    hidden,
    norm_gain,
    expert_choice,
    route_weight,
    gate_weight,
    up_weight,
    down_weight,
    layer_grad,
    scan_input,
    state_input,
    state_output,
    log_decay,
    skip_gain,
    out_weight,
):
    seq_size, head_size = lax.axis_size("seq"), lax.axis_size("head")
    devices = seq_size * head_size
    experts = devices // 2
    tok, model_width = hidden.shape
    top_count = expert_choice.shape[1]
    cap = 9 * tok * top_count // (8 * experts)
    cap = (cap + 7) // 8 * 8
    groups = 1 << ((log2(devices)) // 2)
    plane = devices // groups
    plane_experts = plane // 2
    seq_place, head_place = lax.axis_index("seq"), lax.axis_index("head")
    place = seq_place * head_size + head_place
    group = place // plane

    def across(value, mask):
        return flipped(value, both, mask * plane)

    def spread(first):
        rows = [first]
        for m in range(1, groups):
            low = m & -m
            rows.append(across(rows[m ^ low], low))
        return rows

    chip = (place % plane) // 2

    def within(value, mask):
        return flipped(value, both, 2 * mask)

    seq_rows, inner_width = scan_input.shape
    heads_local = log_decay.shape[1]
    head_dim = inner_width // heads_local
    inner_seq = 1 << (log2(seq_size) // 2)
    outer_seq = seq_size // inner_seq
    inner_place, outer_place = seq_place % inner_seq, seq_place // inner_seq

    choice_t = expert_choice.T
    named = choice_t[None, :, :] == jnp.arange(experts, dtype=jnp.int32)[:, None, None]
    chosen = jnp.any(named, axis=1)
    before = jnp.arange(tok)[:, None] < jnp.arange(tok)[None, :]
    rank = dot_nn(chosen.astype(short), before.astype(short))
    rank = jnp.where(chosen, rank, -1.0).astype(short)
    route_t = route_weight.T.astype(wide)
    prob = jnp.sum(jnp.where(named, route_t[None], 0.0), axis=1).astype(short)
    tables = jnp.concatenate([rank, prob], axis=0)
    pieces = [tables[i : i + 16] for i in range(0, 2 * experts, 16)]
    pieces.append(jnp.zeros((16, model_width - tok * len(pieces)), short))
    table_rows = jnp.concatenate(pieces, axis=1)

    hidden_wide = hidden.astype(wide)
    inverse = lax.rsqrt(jnp.mean(hidden_wide * hidden_wide, axis=1, keepdims=True) + epsilon)
    normalized = hidden_wide * inverse
    normed = (normalized * norm_gain[None, :]).astype(short)
    bundles = spread(jnp.concatenate([normed, layer_grad, table_rows], axis=0))

    gate_up = jnp.concatenate([gate_weight[0], up_weight[0]], axis=1)

    order = jnp.arange(plane_experts, dtype=jnp.int32) ^ chip
    selected = group * plane_experts + order
    own_expert = selected[:1]

    hits, received, returning = [], [], []
    kept = None

    packed = []

    def prepare(m):
        ties = []
        if m == 1:
            ties = [received[0][1]]
        elif m == 2:
            ties = [received[1][1]]
        elif m > 2:
            ties = [*received[m - 2], returning[m - 3][0]]
        sent, hit = pack(selected, bundles[m], cap, tok, experts, ties)
        hits.append(hit)
        packed.append(sent)

    def send(m):
        pieces = [packed[m][0]]
        for k in range(1, plane_experts):
            outgoing = packed[m][k]
            if m == groups - 1 and k == plane_experts - 1:
                outgoing = tied(outgoing, returning[m - 2][0])
            pieces.append(within(outgoing, k))
        received.append(pieces)

    def work(m, kept):
        ties = [hits[m + 2]] if 1 <= m < groups - 2 else []
        rows, kept = expert_rows(own_expert, received[m], weights, m, groups, kept, ties)
        returning.append(rows)
        return kept

    for m in range(min(3, groups)):
        prepare(m)
        send(m)
    weights = [(gate_up, down_weight[0])]
    weights.append(
        (
            flipped(tied(gate_up, *received[0][1:]), "head", 1),
            flipped(tied(down_weight[0], *received[0][1:]), "head", 1),
        )
    )

    lower = jnp.arange(seq_rows)[:, None] >= jnp.arange(seq_rows)[None, :]
    lower_ones = lower.astype(wide)
    cumulative = jnp.dot(lower_ones, log_decay, precision=highest)
    cumulative_t = cumulative.T
    total_decay = cumulative[-1]
    head_of = (jnp.arange(inner_width) // head_dim)[None, :] == jnp.arange(heads_local)[:, None]
    expand = head_of.astype(wide)

    def expanded(value):
        return jnp.dot(value, expand, precision=highest)

    from_start = expanded(jnp.exp(cumulative))
    to_end = expanded(jnp.exp(total_decay[None, :] - cumulative))
    skip_row = expanded(skip_gain[None, :])
    values = scan_input.astype(wide)
    values_end = (values * to_end).astype(short)
    def columns_of(logs, valid):
        factors = jnp.exp(jnp.minimum(jnp.stack(logs, axis=0), 0.0))
        factors = jnp.where(jnp.stack([jnp.asarray(v) for v in valid])[:, None], factors, 0.0)
        return lax.dot_general(
            expand, factors, (((0,), (1,)), ((), ())), precision=highest,
            preferred_element_type=wide,
        )

    def combined(pieces, columns, first, step):
        total = jnp.zeros((inner_width, state_input.shape[1]), wide)
        for k, piece in enumerate(pieces):
            place_of = first + step * k
            total = total + columns[:, place_of : place_of + 1] * piece.astype(wide)
        return total

    def thirds(value, width):
        high = lax.reduce_precision(value, 8, 7)
        middle = lax.reduce_precision(value - high, 8, 7)
        rows = jnp.concatenate([high, middle, value - high - middle], axis=0)
        below = (rows.shape[0] + 15) // 16 * 16 - rows.shape[0]
        return jnp.pad(rows, ((0, below), (0, width - rows.shape[1]))).astype(short)

    def joined_thirds(rows, count, width):
        rows = rows[: 3 * count, :width].astype(wide)
        return rows[:count] + rows[count : 2 * count] + rows[2 * count :]

    start = outer_place * inner_seq
    local_state = tied(dot_tn(values_end, state_input, short), received[0][1])
    message = jnp.concatenate([local_state, thirds(total_decay[None, :], lanes)], axis=0)
    messages = [message] + [flipped(message, "seq", m) for m in range(1, inner_seq)]
    inner_totals = jnp.zeros((inner_seq, heads_local), wide)
    for m in range(inner_seq):
        piece = joined_thirds(messages[m][inner_width:], 1, heads_local)
        inner_totals = lax.dynamic_update_slice(inner_totals, piece, (inner_place ^ m, 0))
    inner_ended = jnp.concatenate(
        [jnp.zeros((1, heads_local), wide), jnp.cumsum(inner_totals, axis=0)], axis=0
    )

    def inner_before(index):
        return lax.dynamic_index_in_dim(inner_ended, index, 0, False)

    logs, valid = [], []
    for m in range(inner_seq):
        source = inner_place ^ m
        logs.append(inner_before(inner_place) - inner_before(source + 1))
        logs.append(inner_before(inner_seq) - inner_before(source + 1))
        valid.extend([source < inner_place, True])
    columns = columns_of(logs, valid)
    states = [v[:inner_width] for v in messages]
    state_in = combined(states, columns, 0, 2)
    for m in range(min(2, groups)):
        if 3 <= m + 2 < groups:
            prepare(m + 2)
        kept = work(m, kept)
        if 3 <= m + 2 < groups:
            send(m + 2)

    message = jnp.concatenate(
        [combined(states, columns, 1, 2).astype(short), thirds(inner_totals, lanes)], axis=0
    )
    message = tied(message, received[-1][1])
    messages = [message] + [flipped(message, "seq", m * inner_seq) for m in range(1, outer_seq)]
    totals = jnp.zeros((seq_size, heads_local), wide)
    for m in range(outer_seq):
        piece = joined_thirds(messages[m][inner_width:], inner_seq, heads_local)
        totals = lax.dynamic_update_slice(totals, piece, ((outer_place ^ m) * inner_seq, 0))
    ended = jnp.concatenate(
        [jnp.zeros((1, heads_local), wide), jnp.cumsum(totals, axis=0)], axis=0
    )

    def before_of(index):
        return lax.dynamic_index_in_dim(ended, jnp.clip(index, 0, seq_size), 0, False)

    logs, valid = [], []
    for m in range(1, outer_seq):
        source = outer_place ^ m
        logs.append(before_of(seq_place) - before_of((source + 1) * inner_seq))
        valid.append(source < outer_place)
    columns = columns_of(logs, valid)
    state_in = state_in + combined([v[:inner_width] for v in messages[1:]], columns, 0, 1)

    logs, valid = [], []
    for m in range(inner_seq):
        source = start + (inner_place ^ m)
        logs.append(before_of(source) - before_of(seq_place + 1))
        logs.append(before_of(source) - before_of(start))
        valid.extend([source > seq_place, True])
    for k in range(1, outer_seq):
        logs.append(before_of(start + k * inner_seq) - before_of(seq_place + 1))
        valid.append(True)
    adjoint_columns = columns_of(logs, valid)

    state_short = state_in.astype(short)
    read_state = dot_nt(state_output, state_short) * from_start
    y_inner = scan_forward(state_input, state_output, scan_input, cumulative_t, cumulative)
    y_rounded = (y_inner + read_state + skip_row * values).astype(short)


    for m in range(2, groups):
        if m + 2 < groups:
            prepare(m + 2)
        kept = work(m, kept)
        if m + 2 < groups:
            send(m + 2)

    partial = [None] * groups
    for m in reversed(range(groups)):
        outgoing = list(returning[m])
        if m < groups - 1:
            after = partial[m + 2] if m < groups - 2 else returning[groups - 1][0]
            outgoing = outgoing[:1] + [tied(v, after) for v in outgoing[1:]]
        back = outgoing[:1] + [within(outgoing[k], k) for k in range(1, plane_experts)]
        partial[m] = dot_tn(hits[m], jnp.concatenate(back, axis=0))

    def sorted_blocks(value):
        width = value.shape[1]
        return jnp.concatenate(
            [
                lax.dynamic_slice(value, ((head_place ^ n) * tok, 0), (tok, width))
                for n in range(head_size)
            ],
            axis=0,
        )

    y_sorted = sorted_blocks(y_rounded)

    other_terms = weight_terms(*kept, 1, (), [partial[0], y_sorted])[0]
    partial[0] = tied(partial[0], other_terms)

    bit = 1
    tree = {m: partial[m] for m in range(groups)}
    while bit < groups:
        moved = {m: across(tree[m].astype(short), bit) for m in tree if m & bit}
        tree = {m: tree[m] + moved[m ^ bit].astype(wide) for m in tree if not m & bit}
        bit = bit * 2
    d_normed = tree[0][:, :model_width]

    prob_tokens = tree[0][:, model_width : model_width + experts].T
    d_route = jnp.sum(jnp.where(named, prob_tokens[:, None, :], 0.0), axis=0)
    d_route_weight = (d_route / route_t).T.astype(short)

    gain_scaled = norm_gain[None, :] * d_normed
    centered = jnp.mean(gain_scaled * normalized, axis=1, keepdims=True)
    d_hidden = (
        layer_grad.astype(wide) + inverse * (gain_scaled - normalized * centered)
    ).astype(short)
    gain_part = jnp.sum(d_normed * normalized, axis=0)

    gain_rows = thirds(gain_part[None, :], model_width)
    blocks = {0: jnp.concatenate([d_hidden, gain_rows], axis=0)}
    for k in reversed(range(log2(head_size))):
        blocks.update({m ^ (1 << k): flipped(v, "head", 1 << k) for m, v in blocks.items()})
    gains = jnp.zeros((head_size, model_width), wide)
    for m, value in blocks.items():
        spot = head_place ^ m
        gains = lax.dynamic_update_slice(gains, joined_thirds(value[tok:], 1, model_width), (spot, 0))
    cotangent = jnp.concatenate([blocks[m][:tok] for m in range(head_size)], axis=0)
    near = head_size // 2
    grad = [
        dot_nn(jnp.concatenate([blocks[m][:tok] for m in part], axis=0), out_weight, short)
        for part in (range(near), range(near, head_size))
    ]
    grad = sorted_blocks(jnp.concatenate(grad, axis=0))
    grad_wide = grad.astype(wide)
    grad_start = (grad_wide * from_start).astype(short)
    local_adjoint = dot_tn(grad_start, state_output, short)

    block = model_width // seq_size
    chosen_cot = {}
    for m in range(inner_seq):
        columns = [
            lax.dynamic_slice(
                cotangent, (0, (o * inner_seq + (inner_place ^ m)) * block), (seq_rows, block)
            )
            for o in range(outer_seq)
        ]
        chosen_cot[m] = jnp.concatenate(columns, axis=1)
    adjoints = [local_adjoint] + [flipped(local_adjoint, "seq", m) for m in range(1, inner_seq)]
    adjoint = combined(adjoints, adjoint_columns, 0, 2)
    joined = combined(adjoints, adjoint_columns, 1, 2).astype(short)
    later = [shifted(joined, "seq", -k * inner_seq) for k in range(1, outer_seq)]
    part_y = tied(y_sorted, local_adjoint)
    sent_products = [dot_tn(part_y, chosen_cot[m], short) for m in range(1, inner_seq)]
    moved = [flipped(v, "seq", m + 1) for m, v in enumerate(sent_products)]
    dx_inner, later_sum, earlier_sum, db_inner, dc_inner = scan_backward(
        state_input, state_output, scan_input, grad, cumulative_t, cumulative,
        sent_products[0], joined,
    )
    other_terms = flipped(tied(other_terms, cotangent), "head", 1)
    product = dot_tn(tied(part_y, joined), chosen_cot[0])
    for value in moved:
        product = product + value.astype(wide)
    adjoint = tied(adjoint, dx_inner) + combined(later, adjoint_columns, 2 * inner_seq, 1)
    adjoint_short = adjoint.astype(short)
    grad_wide = tied(grad, adjoint_short).astype(wide)
    product_short = product.astype(short)
    moved = []
    for m in range(1, outer_seq):
        piece = lax.dynamic_slice(
            product_short, (0, (outer_place ^ m) * block), (inner_width, block)
        )
        moved.append(flipped(piece, "seq", m * inner_seq))

    read_adjoint = dot_nt(state_input, adjoint_short) * to_end
    d_scan_input = (dx_inner + read_adjoint + skip_row * grad_wide).astype(short)
    input_part = db_inner + dot_nn(values_end, adjoint_short)
    output_part = dc_inner + dot_nn((grad_wide * from_start).astype(short), state_short)
    shared = jnp.concatenate([input_part, output_part], axis=0).astype(short)
    d_gate_weight, d_up_weight, d_down_weight = weight_terms(
        *kept, 0, (other_terms,), [shared]
    )
    for k in range(log2(head_size)):
        shared = tied(shared, d_down_weight) if k else shared
        other = flipped(shared, "head", 1 << k)
        shared = shared + other
    shared = shared.astype(wide)
    d_out = lax.dynamic_slice(product, (0, outer_place * block), (inner_width, block))
    d_out = tied(d_out, d_down_weight)
    for value in moved:
        d_out = d_out + value.astype(wide)
    d_out_weight = d_out.T.astype(short)
    d_state_input, d_state_output = shared[:seq_rows], shared[seq_rows:]

    def head_sum(value):
        return jnp.dot(value, expand.T, precision=highest)

    skip_part = jnp.sum(head_sum(values * grad_wide), axis=0)
    skip_part = jnp.pad(skip_part, (0, lanes - heads_local))
    tail_sum = jnp.concatenate([jnp.sum(gains, axis=0), skip_part], axis=0)
    tail_sum = summed(tied(tail_sum, d_down_weight), "seq")
    d_norm_gain = tail_sum[:model_width]
    d_skip_gain = tail_sum[model_width : model_width + heads_local]
    growth = jnp.exp(total_decay)
    from_past = head_sum(read_state * grad_wide)
    to_future = head_sum(read_adjoint * values)
    corner = growth * jnp.sum(
        (state_in * adjoint).reshape(heads_local, head_dim * state_input.shape[1]), axis=1
    )
    forward_part = tied(later_sum.T - earlier_sum + from_past, d_down_weight)
    d_log_decay = (
        lax.dot_general(
            lower_ones, forward_part, (((0,), (0,)), ((), ())),
            precision=highest, preferred_element_type=wide,
        )
        + jnp.dot(lower_ones - jnp.eye(seq_rows, dtype=wide), to_future, precision=highest)
        + corner[None, :]
    )
    return (
        d_hidden,
        d_norm_gain,
        d_route_weight,
        d_gate_weight,
        d_up_weight,
        d_down_weight,
        d_out_weight,
        d_scan_input,
        d_state_input,
        d_state_output,
        d_log_decay,
        d_skip_gain,
    )


def solution(mesh):
    in_specs = (
        P(("seq", "head"), None),
        P(),
        P(("seq", "head"), None),
        P(("seq", "head"), None),
        P(("seq", "head"), None, None),
        P(("seq", "head"), None, None),
        P(("seq", "head"), None, None),
        P(("seq", "head"), None),
        P("seq", "head"),
        P("seq", None),
        P("seq", None),
        P("seq", "head"),
        P("head"),
        P(None, "head"),
    )
    out_specs = (
        P(("seq", "head"), None),
        P(),
        P(("seq", "head"), None),
        P(("seq", "head"), None, None),
        P(("seq", "head"), None, None),
        P(("seq", "head"), None, None),
        P("seq", "head"),
        P("seq", "head"),
        P("seq", None),
        P("seq", None),
        P("seq", "head"),
        P("head"),
    )
    return jax.shard_map(shards, mesh=mesh, in_specs=in_specs, out_specs=out_specs, check_vma=False)
```
